256 devices in a mesh: lon: 16 (over z, x_hi), lat: 8 (over y, x_lo), mem: 2 (over core).
Axes of the slice: x: 4 (x_hi: 2, x_lo: 2; x = x_hi * 2 + x_lo), y: 4, z: 8, core: 2. Of those that a mesh axis runs over, the one named last changes fastest.
Arguments:
- alpha_fields: float32 [2, 10, 512, 1024], P('mem', None, 'lon', 'lat'), may hold values from -6 to 6
- anomalies: float32 [2, 10, 512, 1024], P('mem', None, 'lon', 'lat'), may hold values from -6 to 6
- lon_faces: float32 [10, 512, 1024], P(None, 'lon', 'lat'), may hold values from 0.02 to 0.24
- lat_faces: float32 [10, 512, 1024], P(None, 'lon', 'lat'), may hold values from 0.02 to 0.24
- normalizer: float32 [10, 512, 1024], P(None, 'lon', 'lat'), may hold values from 0.5 to 2
- innovation: float32 [10, 512, 1024], P(None, 'lon', 'lat'), may hold values from -6 to 6
- misfit_weight: float32 [10, 512, 1024], P(None, 'lon', 'lat'), may hold values from 0.3 to 3
- vertical: float32 [10, 10], replicated, may hold values from -0.2 to 1.2
Outputs:
- increment: float32 [10, 512, 1024], P('mem', 'lon', 'lat')
- gradient: float32 [2, 10, 512, 1024], P('mem', None, 'lon', 'lat')
The draws below stay inside these ranges and needn't reach their ends.
All inputs are finite; a program needn't handle non-finite values.
Results may differ from the reference program's by a relative error of at most 0.00015.
Values sent between devices are 32-bit elements; how exact they have to be, the bound alone decides.
No kernel may reach another device: no remote copies, remote signals or barrier semaphores. Data moves between devices by JAX's collectives and lax.ppermute only.
A program may use at most 64 MiB of HBM per device.

```python
import math
import jax
import jax.numpy as jnp
from jax import lax

LEV = 10
STEPS = 8
MEMBERS = 2
NLON = 512
NLAT = 1024


def draw_vertical(key, part):
    key = jax.random.fold_in(key, 11)
    key_diag, key_coupling = jax.random.split(key)
    identity = jnp.eye(LEV, dtype=jnp.float32)
    diagonal_part = jax.random.uniform(key_diag, (LEV, LEV), jnp.float32, 0.9, 1.1)
    coupling = jax.random.uniform(key_coupling, (LEV, LEV), jnp.float32, -0.08, 0.08)
    return identity * diagonal_part + (1.0 - identity) * coupling


def levels(key, shape, pieces, smallest, largest):
    def one(dim, blocks):
        steps = jax.random.uniform(jax.random.fold_in(jax.random.fold_in(key, 6), dim), (blocks,), jnp.float32, smallest / len(pieces), largest / len(pieces))
        return jnp.repeat(jnp.exp(steps), shape[dim] // blocks).reshape((-1,) + (1,) * (len(shape) - dim - 1))

    level = one(*pieces[0])
    for cut in pieces[1:]:
        level = level * one(*cut)
    return level


def noise(rng, dims, spread, most, cuts=(), kind=jnp.bfloat16):
    entries = jax.random.normal(rng, dims, jnp.float32) * spread
    if len(cuts) > 0:
        entries = levels(rng, dims, cuts, -0.22, 0.18) * entries
    return jnp.clip(entries, min=-most, max=most).astype(kind)


def setup_inputs(seed: int = 0) -> dict:
    seeds = jax.random.split(jax.random.key(seed), 9)
    return {
        "alpha_fields": noise(seeds[0], (MEMBERS, LEV, NLON, NLAT), 1.0, 6.0, ((0, 2), (2, 16), (3, 8)), jnp.float32),
        "anomalies": noise(seeds[1], (MEMBERS, LEV, NLON, NLAT), 1.0, 6.0, ((0, 2), (2, 16), (3, 8)), jnp.float32),
        "lon_faces": jnp.clip(jnp.exp(math.log(0.24) - 2.4849066 * jax.random.uniform(seeds[2], (LEV, NLON, NLAT), jnp.float32) ** levels(seeds[2], (LEV, NLON, NLAT), ((1, 16), (2, 8)), -0.2, 0.2)), 0.02, 0.24),
        "lat_faces": jnp.clip(jnp.exp(math.log(0.24) - 2.4849066 * jax.random.uniform(seeds[3], (LEV, NLON, NLAT), jnp.float32) ** levels(seeds[3], (LEV, NLON, NLAT), ((1, 16), (2, 8)), -0.2, 0.2)), 0.02, 0.24),
        "normalizer": jnp.clip(jnp.exp(math.log(2.0) - 1.3862944 * jax.random.uniform(seeds[4], (LEV, NLON, NLAT), jnp.float32) ** levels(seeds[4], (LEV, NLON, NLAT), ((1, 16), (2, 8)), -0.2, 0.2)), 0.5, 2.0),
        "innovation": noise(seeds[5], (LEV, NLON, NLAT), 1.0, 6.0, ((1, 16), (2, 8)), jnp.float32),
        "misfit_weight": jnp.clip(jnp.exp(math.log(3.0) - 2.3025851 * jax.random.uniform(seeds[6], (LEV, NLON, NLAT), jnp.float32) ** levels(seeds[6], (LEV, NLON, NLAT), ((1, 16), (2, 8)), -0.2, 0.2)), 0.3, 3.0),
        "vertical": draw_vertical(jax.random.fold_in(seeds[8], 71), 0),
    }


def pad_edges(field):
    field = jnp.concatenate([field[..., -1:, :], field, field[..., :1, :]], axis=-2)
    zeros = jnp.zeros(field.shape[:-1] + (1,), field.dtype)
    return jnp.concatenate([zeros, field, zeros], axis=-1)

def smooth_step(field, lon_coef, lat_coef):
    flux_x = lon_coef[..., :-1, :] * (field[..., 1:, :] - field[..., :-1, :])
    flux_y = lat_coef[..., :, :-1] * (field[..., :, 1:] - field[..., :, :-1])
    return field[..., 1:-1, 1:-1] + (flux_x[..., 1:, 1:-1] - flux_x[..., :-1, 1:-1]) + (flux_y[..., 1:-1, 1:] - flux_y[..., 1:-1, :-1])

def diffuse(field, lon_padded, lat_padded):
    for sweep_index in range(STEPS):
        field = smooth_step(pad_edges(field), lon_padded, lat_padded)
    return field

def reference(alpha_fields, anomalies, lon_faces, lat_faces, normalizer, innovation, misfit_weight, vertical):
    members = alpha_fields.shape[0]
    member_scale = 1.0 / math.sqrt(members - 1)
    inside = (jnp.arange(NLAT) < NLAT - 1).astype(lat_faces.dtype)
    lon_padded = pad_edges(lon_faces)
    lat_padded = pad_edges(lat_faces * inside)

    def forward(running, member_pair):
        alpha_one, anomaly_one = member_pair
        vertical_mixed = jnp.einsum('lk,kxy->lxy', vertical, alpha_one, precision=lax.Precision.HIGHEST)
        localized = normalizer * diffuse(vertical_mixed, lon_padded, lat_padded)
        return (running + anomaly_one * localized, None)
    summed, _ = lax.scan(forward, jnp.zeros_like(normalizer), (alpha_fields, anomalies))
    increment = member_scale * summed
    misfit = misfit_weight * (increment - innovation)

    def backward(member_pair):
        alpha_one, anomaly_one = member_pair
        adjoint_field = diffuse(normalizer * anomaly_one * misfit, lon_padded, lat_padded)
        return alpha_one + member_scale * jnp.einsum('kl,kxy->lxy', vertical, adjoint_field, precision=lax.Precision.HIGHEST)
    gradient = lax.map(backward, (alpha_fields, anomalies))
    return (increment, gradient)
```

```python
import functools
import math

import jax
import jax.numpy as jnp
from jax import lax
from jax.experimental import pallas as pl
from jax.experimental.pallas import tpu as pltpu
from jax.sharding import PartitionSpec as P

STEPS = 8
DEEP = 2 * STEPS
LANES = 128
VMEM = pl.BlockSpec(memory_space=pltpu.VMEM)
SMEM = pl.BlockSpec(memory_space=pltpu.SMEM)
PARAMS = pltpu.CompilerParams(vmem_limit_bytes=32 * 1024 * 1024)


def f32(*shape):
    return jax.ShapeDtypeStruct(shape, jnp.float32)


def around(value, axis, steps):
    count = lax.axis_size(axis)
    pairs = [(source, (source + steps) % count) for source in range(count)]
    return lax.ppermute(value, axis, pairs)


def lane_places(deep, shallow):
    at = 0
    places = []
    for width, count in ((DEEP, deep), (STEPS, shallow)):
        for _ in range(count):
            places.append((at // LANES, at % LANES, width))
            at += width
    return places, -(-at // LANES)


def mixed(vertical_ref, alpha_ref, level):
    total = vertical_ref[level, 0] * alpha_ref[0, 0]
    for k in range(1, alpha_ref.shape[1]):
        total = total + vertical_ref[level, k] * alpha_ref[0, k]
    return total


def prepare_kernel(
    half, vertical, alpha, anomaly, lon_faces, lat_faces, normalizer, innovation, weight, keep, give
):
    base = lax.axis_index("mem") * half
    other = half - base
    last = lax.axis_index("lat") == lax.axis_size("lat") - 1
    lane = lax.broadcasted_iota(jnp.int32, lon_faces.shape[1:], 1)
    closed = jnp.logical_and(last, lane == lon_faces.shape[2] - 1)
    for i in range(half):
        mine, theirs = base + i, other + i
        root = jnp.sqrt(weight[mine])
        keep[i] = mixed(vertical, alpha, mine)
        keep[half + i] = lon_faces[mine]
        keep[2 * half + i] = jnp.where(closed, 0.0, lat_faces[mine])
        keep[3 * half + i] = normalizer[mine] * anomaly[0, mine] * root
        keep[4 * half + i] = root * innovation[mine]
        keep[5 * half + i] = 1.0 / root
        give[i] = mixed(vertical, alpha, theirs)
        give[half + i] = normalizer[theirs] * anomaly[0, theirs] * jnp.sqrt(weight[theirs])


def field_refs(half, keep, got):
    deep = [keep.at[i] for i in range(half)]
    deep += [got.at[i] for i in range(half)]
    deep += [keep.at[half + i] for i in range(2 * half)]
    shallow = [keep.at[3 * half + i] for i in range(half)]
    shallow += [got.at[half + i] for i in range(half)]
    shallow += [keep.at[4 * half + i] for i in range(half)]
    return deep, shallow


def lon_pack_kernel(half, keep, got, first, final):
    deep, shallow = field_refs(half, keep, got)
    rows = keep.shape[1]
    at = 0
    for width, fields in ((DEEP, deep), (STEPS, shallow)):
        for ref in fields:
            first[at : at + width] = ref[:width]
            final[at : at + width] = ref[rows - width :]
            at += width


def lat_pack_kernel(half, keep, got, below, above, deep_out, shallow_out, first, final):
    deep, shallow = field_refs(half, keep, got)
    rows, lanes = keep.shape[1:]
    places, _ = lane_places(len(deep), len(shallow))
    first[...] = jnp.zeros_like(first)
    final[...] = jnp.zeros_like(final)
    lane = lax.broadcasted_iota(jnp.int32, (1, lanes), 1)
    at = 0
    index = 0
    for width, fields, out in ((DEEP, deep, deep_out), (STEPS, shallow, shallow_out)):
        start = DEEP - width
        stop = rows + DEEP + width
        for i, ref in enumerate(fields):
            out[i, :width] = below[at : at + width]
            out[i, width : width + rows] = ref[...]
            out[i, width + rows :] = above[at : at + width]
            at += width
            group, place, _ = places[index]
            index += 1
            block = out[i]
            inside = jnp.logical_and(lane >= place, lane < place + width)
            head = pltpu.roll(block, place, axis=1) if place else block
            shift = (place + width) % lanes
            tail = pltpu.roll(block, shift, axis=1) if shift else block
            first[group, start:stop] = jnp.where(inside, head, first[group, start:stop])
            final[group, start:stop] = jnp.where(inside, tail, final[group, start:stop])


def diffusion_step(field, lon_coef, lat_coef):
    rows, lanes = field.shape
    flux_x = lon_coef * (pltpu.roll(field, rows - 1, axis=0) - field)
    flux_y = lat_coef * (pltpu.roll(field, lanes - 1, axis=1) - field)
    return (
        field
        + (flux_x - pltpu.roll(flux_x, 1, axis=0))
        + (flux_y - pltpu.roll(flux_y, 1, axis=1))
    )


def diffuse_kernel(
    half, deep, shallow, keep, left, right, increment, mine, theirs, deep_side, shallow_side
):
    lanes = deep.shape[2]
    rows = keep.shape[1]
    places, _ = lane_places(deep.shape[0], shallow.shape[0])
    lane = lax.broadcasted_iota(jnp.int32, (1, lanes), 1)
    index = 0
    for width, side in ((DEEP, deep_side), (STEPS, shallow_side)):
        start = DEEP - width
        stop = rows + DEEP + width
        for i in range(side.shape[0]):
            group, place, _ = places[index]
            index += 1
            after = pltpu.roll(right[group, start:stop], (lanes - place) % lanes, axis=1)
            before = pltpu.roll(left[group, start:stop], (2 * lanes - width - place) % lanes, axis=1)
            side[i] = jnp.where(
                lane < width, after, jnp.where(lane >= lanes - width, before, 0.0)
            )

    def level(i, carry):
        def deep_field(n):
            return jnp.concatenate([deep[n * half + i], deep_side[n * half + i]], axis=1)

        def shallow_field(n):
            return jnp.concatenate([shallow[n * half + i], shallow_side[n * half + i]], axis=1)

        cut = DEEP - STEPS
        lon_coef, lat_coef = deep_field(2), deep_field(3)
        roots = []
        for n in range(2):
            field = deep_field(n)
            for _ in range(STEPS):
                field = diffusion_step(field, lon_coef, lat_coef)
            roots.append(field[cut:-cut])
        gains = [shallow_field(0), shallow_field(1)]
        total = gains[0] * roots[0] + gains[1] * roots[1]
        increment[i] = total[STEPS : STEPS + rows, :lanes] * keep[5 * half + i]
        residual = total - shallow_field(2)
        lon_coef, lat_coef = lon_coef[cut:-cut], lat_coef[cut:-cut]
        for gain, out in zip(gains, (mine, theirs)):
            field = gain * residual
            for _ in range(STEPS):
                field = diffusion_step(field, lon_coef, lat_coef)
            out[i] = field[STEPS : STEPS + rows, :lanes]
        return carry

    lax.fori_loop(0, half, level, 0)


def gradient_kernel(half, vertical, alpha, mine, got, gradient):
    base = lax.axis_index("mem") * half
    other = half - base
    for k in range(2 * half):
        total = alpha[0, k]
        for i in range(half):
            total = total + vertical[base + i, k] * mine[i]
            total = total + vertical[other + i, k] * got[i]
        gradient[0, k] = total


def local(
    alpha_fields, anomalies, lon_faces, lat_faces, normalizer, innovation, misfit_weight, vertical
):
    levels, rows, lanes = lon_faces.shape
    half = levels // 2
    deep_count, shallow_count = 4 * half, 3 * half
    _, groups = lane_places(deep_count, shallow_count)
    pack_rows = DEEP * deep_count + STEPS * shallow_count
    deep_shape = (deep_count, rows + 2 * DEEP, lanes)
    shallow_shape = (shallow_count, rows + 2 * STEPS, lanes)

    keep, give = pl.pallas_call(
        functools.partial(prepare_kernel, half),
        out_shape=(f32(6 * half, rows, lanes), f32(levels, rows, lanes)),
        in_specs=[SMEM] + [VMEM] * 7,
        out_specs=(VMEM, VMEM),
        compiler_params=PARAMS,
        name="prepare",
    )(vertical, alpha_fields, anomalies, lon_faces, lat_faces, normalizer, innovation, misfit_weight)
    got = around(give, "mem", 1)

    first, final = pl.pallas_call(
        functools.partial(lon_pack_kernel, half),
        out_shape=(f32(pack_rows, lanes), f32(pack_rows, lanes)),
        in_specs=[VMEM] * 2,
        out_specs=(VMEM, VMEM),
        compiler_params=PARAMS,
        name="lon_pack",
    )(keep, got)
    below = around(final, "lon", 1)
    above = around(first, "lon", -1)

    pack_shape = f32(groups, rows + 2 * DEEP, lanes)
    deep, shallow, first, final = pl.pallas_call(
        functools.partial(lat_pack_kernel, half),
        out_shape=(f32(*deep_shape), f32(*shallow_shape), pack_shape, pack_shape),
        in_specs=[VMEM] * 4,
        out_specs=(VMEM,) * 4,
        compiler_params=PARAMS,
        name="lat_pack",
    )(keep, got, below, above)
    left = around(final, "lat", 1)
    right = around(first, "lat", -1)

    block = f32(half, rows, lanes)
    increment, mine, theirs = pl.pallas_call(
        functools.partial(diffuse_kernel, half),
        out_shape=(block, block, block),
        in_specs=[VMEM] * 5,
        out_specs=(VMEM,) * 3,
        scratch_shapes=[
            pltpu.VMEM(deep_shape, jnp.float32),
            pltpu.VMEM(shallow_shape, jnp.float32),
        ],
        compiler_params=PARAMS,
        name="diffuse",
    )(deep, shallow, keep, left, right)
    got = around(theirs, "mem", 1)

    gradient = pl.pallas_call(
        functools.partial(gradient_kernel, half),
        out_shape=f32(*alpha_fields.shape),
        in_specs=[SMEM] + [VMEM] * 3,
        out_specs=VMEM,
        compiler_params=PARAMS,
        name="gradient",
    )(vertical, alpha_fields, mine, got)
    return (increment, gradient)


def solution(mesh):
    return jax.shard_map(
        local,
        mesh=mesh,
        in_specs=(
            P("mem", None, "lon", "lat"),
            P("mem", None, "lon", "lat"),
            P(None, "lon", "lat"),
            P(None, "lon", "lat"),
            P(None, "lon", "lat"),
            P(None, "lon", "lat"),
            P(None, "lon", "lat"),
            P(),
        ),
        out_specs=(P("mem", "lon", "lat"), P("mem", None, "lon", "lat")),
        check_vma=False,
    )
```

```python
import functools
import math

import jax
import jax.numpy as jnp
from jax import lax
from jax.experimental import pallas as pl
from jax.experimental.pallas import tpu as pltpu
from jax.sharding import PartitionSpec as P

STEPS = 8
DEEP = 2 * STEPS
LANES = 128
VMEM = pl.BlockSpec(memory_space=pltpu.VMEM)
SMEM = pl.BlockSpec(memory_space=pltpu.SMEM)
HBM = pl.BlockSpec(memory_space=pltpu.HBM)
PARAMS = pltpu.CompilerParams(vmem_limit_bytes=32 * 1024 * 1024)


def f32(*shape):
    return jax.ShapeDtypeStruct(shape, jnp.float32)


def around(value, axis, steps):
    count = lax.axis_size(axis)
    pairs = [(source, (source + steps) % count) for source in range(count)]
    return lax.ppermute(value, axis, pairs)


def diagonal(value, lon_steps, lat_steps):
    lons, lats = lax.axis_size("lon"), lax.axis_size("lat")
    pairs = []
    for i in range(lons):
        for j in range(lats):
            target = ((i + lon_steps) % lons) * lats + (j + lat_steps) % lats
            pairs.append((i * lats + j, target))
    return lax.ppermute(value, ("lon", "lat"), pairs)


def lane_places(count, width):
    return [(i * width // LANES, i * width % LANES) for i in range(count)]


def lane_groups(count, width):
    return -(-count * width // LANES)


def turned(value, shift):
    shift = shift % value.shape[-1]
    return pltpu.roll(value, shift, axis=value.ndim - 1) if shift else value


def mixed(vertical_ref, alpha_ref, level):
    total = vertical_ref[level, 0] * alpha_ref[0, 0]
    for k in range(1, alpha_ref.shape[1]):
        total = total + vertical_ref[level, k] * alpha_ref[0, k]
    return total


def prepare_kernel(
    half,
    vertical_hbm,
    alpha_hbm,
    anomaly_hbm,
    lon_hbm,
    lat_hbm,
    normalizer_hbm,
    innovation_hbm,
    weight_hbm,
    keep,
    give,
    vertical,
    alpha,
    anomaly,
    faces,
    normalizer,
    innovation,
    weight,
    sems,
):
    base = lax.axis_index("mem") * half
    other = half - base
    pairs = [
        (vertical_hbm, vertical),
        (alpha_hbm, alpha),
        (weight_hbm, weight),
        (normalizer_hbm, normalizer),
        (anomaly_hbm, anomaly),
        (innovation_hbm.at[pl.ds(base, half)], innovation),
        (lon_hbm.at[pl.ds(base, half)], keep.at[pl.ds(half, half)]),
        (lat_hbm.at[pl.ds(base, half)], faces),
    ]
    copies = [pltpu.make_async_copy(a, b, sems.at[n]) for n, (a, b) in enumerate(pairs)]
    for copy in copies:
        copy.start()
    copies[0].wait()
    copies[1].wait()
    for i in range(half):
        keep[i] = mixed(vertical, alpha, base + i)
        give[i] = mixed(vertical, alpha, other + i)
    for copy in copies[2:]:
        copy.wait()
    last = lax.axis_index("lat") == lax.axis_size("lat") - 1
    lane = lax.broadcasted_iota(jnp.int32, faces.shape[1:], 1)
    closed = jnp.logical_and(last, lane == faces.shape[2] - 1)
    for i in range(half):
        mine, theirs = base + i, other + i
        root = jnp.sqrt(weight[mine])
        keep[2 * half + i] = jnp.where(closed, 0.0, faces[i])
        keep[3 * half + i] = normalizer[mine] * anomaly[0, mine] * root
        keep[4 * half + i] = root * innovation[i]
        keep[5 * half + i] = 1.0 / root
        give[half + i] = normalizer[theirs] * anomaly[0, theirs] * jnp.sqrt(weight[theirs])


def field_refs(half, keep, got):
    deep = [keep.at[i] for i in range(half)]
    deep += [got.at[i] for i in range(half)]
    deep += [keep.at[half + i] for i in range(2 * half)]
    shallow = [keep.at[3 * half + i] for i in range(half)]
    shallow += [got.at[half + i] for i in range(half)]
    shallow += [keep.at[4 * half + i] for i in range(half)]
    return deep, shallow


def pack_kernel(
    half, keep, got, first, final, west, east, west_first, west_final, east_first, east_final
):
    deep, shallow = field_refs(half, keep, got)
    rows, lanes = keep.shape[1:]
    at = 0
    for width, fields in ((DEEP, deep), (STEPS, shallow)):
        for ref in fields:
            first[at : at + width] = ref[:width]
            final[at : at + width] = ref[rows - width :]
            at += width
    lane = lax.broadcasted_iota(jnp.int32, (1, lanes), 1)
    group = -1
    for width, fields in ((DEEP, deep), (STEPS, shallow)):
        per = lanes // width
        for begin in range(0, len(fields), per):
            group += 1
            heads = tails = jnp.zeros((rows, lanes), jnp.float32)
            for slot, ref in enumerate(fields[begin : begin + per]):
                place = slot * width
                inside = jnp.logical_and(lane >= place, lane < place + width)
                block = ref[...]
                heads = jnp.where(inside, turned(block, place), heads)
                tails = jnp.where(inside, turned(block, place + width), tails)
            west[group] = heads
            east[group] = tails
            at = group * DEEP
            west_first[at : at + width] = heads[:width]
            west_final[at : at + width] = heads[rows - width :]
            east_first[at : at + width] = tails[:width]
            east_final[at : at + width] = tails[rows - width :]


def diffuse_kernel(
    half,
    keep,
    got,
    below,
    above,
    left,
    right,
    left_below,
    left_above,
    right_below,
    right_above,
    increment,
    mine,
    theirs,
    deep_tiles,
    shallow_tiles,
    coef,
    work,
):
    deep, shallow = field_refs(half, keep, got)
    rows, lanes = keep.shape[1:]
    lane = lax.broadcasted_iota(jnp.int32, (1, lanes), 1)
    at = 0
    first_group = 0
    for width, fields, tiles in ((DEEP, deep, deep_tiles), (STEPS, shallow, shallow_tiles)):
        for i, (ref, (group, place)) in enumerate(zip(fields, lane_places(len(fields), width))):
            group += first_group
            corner = group * DEEP
            pieces = (
                (below[at : at + width], left_below, right_below, 0, width),
                (ref[...], left, right, width, rows),
                (above[at : at + width], left_above, right_above, width + rows, width),
            )
            at += width
            for block, lefts, rights, start, count in pieces:
                if lefts is left:
                    before, after = left[group], right[group]
                else:
                    before = lefts[corner : corner + width]
                    after = rights[corner : corner + width]
                before = turned(before, DEEP - width - place)
                after = turned(after, lanes - DEEP - place)
                out = slice(STEPS + start, STEPS + start + count)
                tiles[i, 0, out] = jnp.where(lane < DEEP, before, turned(block, DEEP))
                tiles[i, 1, out] = jnp.where(lane >= lanes - DEEP, after, turned(block, -DEEP))
        first_group += lane_groups(len(fields), width)

    high = rows + 2 * DEEP
    edge = jnp.zeros((STEPS, lanes), jnp.float32)
    for n in range(work.shape[0]):
        for t in range(2):
            work[n, t, :STEPS] = edge
            work[n, t, STEPS + high :] = edge
    for n in range(2 * half):
        for t in range(2):
            deep_tiles[2 * half + n, t, :STEPS] = edge

    def sweep(source, target, begin, count, tile, member):
        def at(shift):
            return work[source + member, tile, pl.ds(STEPS + begin + shift, count)]

        def c(n):
            return coef[n, tile, pl.ds(begin, count)]

        here = at(0)
        work[target + member, tile, pl.ds(STEPS + begin, count)] = (
            (c(0) * here + c(1) * at(1))
            + (c(2) * at(-1) + c(3) * turned(here, -1))
            + c(4) * turned(here, 1)
        )

    def sweeps(margin):
        source, target = 0, 2
        for step in range(1, STEPS + 1):
            cut = (margin + step) // 4 * 4
            for tile in range(2):
                for member in range(2):
                    sweep(source, target, cut, high - 2 * cut, tile, member)
            source, target = target, source

    def level(i, carry):
        for tile in range(2):
            body = pl.ds(STEPS, high)
            north = deep_tiles[2 * half + i, tile, body]
            south = deep_tiles[2 * half + i, tile, pl.ds(STEPS - 1, high)]
            east = deep_tiles[3 * half + i, tile, body]
            west = turned(east, 1)
            coef[0, tile] = 1.0 - ((north + south) + (east + west))
            coef[1, tile] = north
            coef[2, tile] = south
            coef[3, tile] = east
            coef[4, tile] = west
            for member in range(2):
                work[member, tile, body] = deep_tiles[member * half + i, tile, body]
        sweeps(0)
        inner = pl.ds(2 * STEPS, high - 2 * STEPS)
        shallow_rows = pl.ds(STEPS, high - 2 * STEPS)
        center = slice(STEPS, STEPS + rows)
        totals = []
        for tile in range(2):
            gains = [shallow_tiles[m * half + i, tile, shallow_rows] for m in range(2)]
            total = gains[0] * work[0, tile, inner] + gains[1] * work[1, tile, inner]
            totals.append(total[center])
            residual = total - shallow_tiles[2 * half + i, tile, shallow_rows]
            for member in range(2):
                work[member, tile, inner] = gains[member] * residual
        joined = lane < lanes // 2
        total = jnp.where(joined, turned(totals[0], -DEEP), turned(totals[1], DEEP))
        increment[i] = total * keep[5 * half + i]
        sweeps(STEPS)
        own = pl.ds(STEPS + DEEP, rows)
        for member, out in enumerate((mine, theirs)):
            parts = [work[member, tile, own] for tile in range(2)]
            out[i] = jnp.where(joined, turned(parts[0], -DEEP), turned(parts[1], DEEP))
        return carry

    lax.fori_loop(0, half, level, 0)


def gradient_kernel(half, vertical, alpha, mine, got, gradient):
    base = lax.axis_index("mem") * half
    other = half - base
    for k in range(2 * half):
        total = alpha[0, k]
        for i in range(half):
            total = total + vertical[base + i, k] * mine[i]
            total = total + vertical[other + i, k] * got[i]
        gradient[0, k] = total


def local(
    alpha_fields, anomalies, lon_faces, lat_faces, normalizer, innovation, misfit_weight, vertical
):
    levels, rows, lanes = lon_faces.shape
    half = levels // 2
    deep_count, shallow_count = 4 * half, 3 * half
    deep_groups = lane_groups(deep_count, DEEP)
    groups = deep_groups + lane_groups(shallow_count, STEPS)
    strip = f32(DEEP * deep_count + STEPS * shallow_count, lanes)
    column = f32(groups, rows, lanes)
    corner = f32(DEEP * deep_groups + STEPS * (groups - deep_groups), lanes)
    block = f32(half, rows, lanes)
    high = rows + 2 * DEEP

    keep, give = pl.pallas_call(
        functools.partial(prepare_kernel, half),
        out_shape=(f32(6 * half, rows, lanes), f32(levels, rows, lanes)),
        in_specs=[HBM] * 8,
        out_specs=(VMEM, VMEM),
        scratch_shapes=[
            pltpu.SMEM(vertical.shape, jnp.float32),
            pltpu.VMEM(alpha_fields.shape, jnp.float32),
            pltpu.VMEM(anomalies.shape, jnp.float32),
            pltpu.VMEM(block.shape, jnp.float32),
            pltpu.VMEM(normalizer.shape, jnp.float32),
            pltpu.VMEM(block.shape, jnp.float32),
            pltpu.VMEM(misfit_weight.shape, jnp.float32),
            pltpu.SemaphoreType.DMA((8,)),
        ],
        compiler_params=PARAMS,
        name="prepare",
    )(vertical, alpha_fields, anomalies, lon_faces, lat_faces, normalizer, innovation, misfit_weight)
    got = around(give, "mem", 1)

    first, final, west, east, west_first, west_final, east_first, east_final = pl.pallas_call(
        functools.partial(pack_kernel, half),
        out_shape=(strip, strip, column, column, corner, corner, corner, corner),
        in_specs=[VMEM] * 2,
        out_specs=(VMEM,) * 8,
        compiler_params=PARAMS,
        name="pack",
    )(keep, got)
    below = around(final, "lon", 1)
    above = around(first, "lon", -1)
    left = around(east, "lat", 1)
    right = around(west, "lat", -1)
    left_below = diagonal(east_final, 1, 1)
    left_above = diagonal(east_first, -1, 1)
    right_below = diagonal(west_final, 1, -1)
    right_above = diagonal(west_first, -1, -1)

    increment, mine, theirs = pl.pallas_call(
        functools.partial(diffuse_kernel, half),
        out_shape=(block, block, block),
        in_specs=[VMEM] * 10,
        out_specs=(VMEM,) * 3,
        scratch_shapes=[
            pltpu.VMEM((deep_count, 2, STEPS + high, lanes), jnp.float32),
            pltpu.VMEM((shallow_count, 2, high, lanes), jnp.float32),
            pltpu.VMEM((5, 2, high, lanes), jnp.float32),
            pltpu.VMEM((4, 2, high + 2 * STEPS, lanes), jnp.float32),
        ],
        compiler_params=PARAMS,
        name="diffuse",
    )(keep, got, below, above, left, right, left_below, left_above, right_below, right_above)
    got = around(theirs, "mem", 1)

    gradient = pl.pallas_call(
        functools.partial(gradient_kernel, half),
        out_shape=f32(*alpha_fields.shape),
        in_specs=[SMEM] + [VMEM] * 3,
        out_specs=VMEM,
        compiler_params=PARAMS,
        name="gradient",
    )(vertical, alpha_fields, mine, got)
    return (increment, gradient)


def solution(mesh):
    return jax.shard_map(
        local,
        mesh=mesh,
        in_specs=(
            P("mem", None, "lon", "lat"),
            P("mem", None, "lon", "lat"),
            P(None, "lon", "lat"),
            P(None, "lon", "lat"),
            P(None, "lon", "lat"),
            P(None, "lon", "lat"),
            P(None, "lon", "lat"),
            P(),
        ),
        out_specs=(P("mem", "lon", "lat"), P("mem", None, "lon", "lat")),
        check_vma=False,
    )
```

```python
import functools
import math

import jax
import jax.numpy as jnp
from jax import lax
from jax.experimental import pallas as pl
from jax.experimental.pallas import tpu as pltpu
from jax.sharding import PartitionSpec as P

STEPS = 8
DEEP = 2 * STEPS
LANES = 128
VMEM = pl.BlockSpec(memory_space=pltpu.VMEM)
SMEM = pl.BlockSpec(memory_space=pltpu.SMEM)
HBM = pl.BlockSpec(memory_space=pltpu.HBM)
PARAMS = pltpu.CompilerParams(vmem_limit_bytes=32 * 1024 * 1024)


def f32(*shape):
    return jax.ShapeDtypeStruct(shape, jnp.float32)


def around(value, axis, steps):
    count = lax.axis_size(axis)
    pairs = [(source, (source + steps) % count) for source in range(count)]
    return lax.ppermute(value, axis, pairs)


def lane_places(count, width):
    return [(i * width // LANES, i * width % LANES) for i in range(count)]


def lane_groups(count, width):
    return -(-count * width // LANES)


def turned(value, shift):
    shift = shift % value.shape[-1]
    return pltpu.roll(value, shift, axis=value.ndim - 1) if shift else value


def mixed(vertical_ref, alpha_ref, level):
    total = vertical_ref[level, 0] * alpha_ref[0, 0]
    for k in range(1, alpha_ref.shape[1]):
        total = total + vertical_ref[level, k] * alpha_ref[0, k]
    return total


def prepare_kernel(
    half,
    vertical_hbm,
    alpha_hbm,
    anomaly_hbm,
    lon_hbm,
    lat_hbm,
    normalizer_hbm,
    innovation_hbm,
    weight_hbm,
    keep,
    give,
    alpha,
    vertical,
    anomaly,
    faces,
    normalizer,
    innovation,
    weight,
    sems,
):
    base = lax.axis_index("mem") * half
    other = half - base
    pairs = [
        (vertical_hbm, vertical),
        (alpha_hbm, alpha),
        (weight_hbm, weight),
        (normalizer_hbm, normalizer),
        (anomaly_hbm, anomaly),
        (innovation_hbm.at[pl.ds(base, half)], innovation),
        (lon_hbm.at[pl.ds(base, half)], keep.at[pl.ds(half, half)]),
        (lat_hbm.at[pl.ds(base, half)], faces),
    ]
    copies = [pltpu.make_async_copy(a, b, sems.at[n]) for n, (a, b) in enumerate(pairs)]
    for copy in copies:
        copy.start()
    copies[0].wait()
    copies[1].wait()
    for i in range(half):
        keep[i] = mixed(vertical, alpha, base + i)
        give[i] = mixed(vertical, alpha, other + i)
    for copy in copies[2:]:
        copy.wait()
    last = lax.axis_index("lat") == lax.axis_size("lat") - 1
    lane = lax.broadcasted_iota(jnp.int32, faces.shape[1:], 1)
    closed = jnp.logical_and(last, lane == faces.shape[2] - 1)
    for i in range(half):
        mine, theirs = base + i, other + i
        root = jnp.sqrt(weight[mine])
        keep[2 * half + i] = jnp.where(closed, 0.0, faces[i])
        keep[3 * half + i] = normalizer[mine] * anomaly[0, mine] * root
        keep[4 * half + i] = root * innovation[i]
        keep[5 * half + i] = 1.0 / root
        give[half + i] = normalizer[theirs] * anomaly[0, theirs] * jnp.sqrt(weight[theirs])


def field_refs(half, keep, got):
    deep = [keep.at[i] for i in range(half)]
    deep += [got.at[i] for i in range(half)]
    deep += [keep.at[half + i] for i in range(2 * half)]
    shallow = [keep.at[3 * half + i] for i in range(half)]
    shallow += [got.at[half + i] for i in range(half)]
    shallow += [keep.at[4 * half + i] for i in range(half)]
    return deep, shallow


def pack_kernel(half, keep, got, first, final, west, east):
    deep, shallow = field_refs(half, keep, got)
    rows, lanes = keep.shape[1:]
    at = 0
    for width, fields in ((DEEP, deep), (STEPS, shallow)):
        for ref in fields:
            first[at : at + width] = ref[:width]
            final[at : at + width] = ref[rows - width :]
            at += width
    lane = lax.broadcasted_iota(jnp.int32, (1, lanes), 1)
    group = -1
    for width, fields in ((DEEP, deep), (STEPS, shallow)):
        per = lanes // width
        for begin in range(0, len(fields), per):
            group += 1
            heads = tails = jnp.zeros((rows, lanes), jnp.float32)
            for slot, ref in enumerate(fields[begin : begin + per]):
                place = slot * width
                inside = jnp.logical_and(lane >= place, lane < place + width)
                block = ref[...]
                heads = jnp.where(inside, turned(block, place), heads)
                tails = jnp.where(inside, turned(block, place + width), tails)
            west[group] = heads
            east[group] = tails


def corner_kernel(deep_groups, left, right, first, final):
    groups, rows = left.shape[:2]
    at = 0
    for column in (left, right):
        for group in range(groups):
            width = DEEP if group < deep_groups else STEPS
            first[at : at + width] = column[group, :width]
            final[at : at + width] = column[group, rows - width :]
            at += width


def diffuse_kernel(
    half,
    keep,
    got,
    below,
    above,
    left,
    right,
    corner_below,
    corner_above,
    increment,
    mine,
    theirs,
    deep_tiles,
    shallow_tiles,
    work,
    flux,
):
    deep, shallow = field_refs(half, keep, got)
    rows, lanes = keep.shape[1:]
    lane = lax.broadcasted_iota(jnp.int32, (1, lanes), 1)
    at = 0
    first_group = 0
    right_corner = corner_below.shape[0] // 2
    for width, fields, tiles in ((DEEP, deep, deep_tiles), (STEPS, shallow, shallow_tiles)):
        for i, (ref, (group, place)) in enumerate(zip(fields, lane_places(len(fields), width))):
            group += first_group
            corner = group * DEEP
            pieces = (
                (below[at : at + width], corner_below, 0, width),
                (ref[...], None, width, rows),
                (above[at : at + width], corner_above, width + rows, width),
            )
            at += width
            for block, corners, start, count in pieces:
                if corners is None:
                    before, after = left[group], right[group]
                else:
                    before = corners[corner : corner + width]
                    after = corners[right_corner + corner : right_corner + corner + width]
                before = turned(before, DEEP - width - place)
                after = turned(after, lanes - DEEP - place)
                out = slice(STEPS + start, STEPS + start + count)
                tiles[i, 0, out] = jnp.where(lane < DEEP, before, turned(block, DEEP))
                tiles[i, 1, out] = jnp.where(lane >= lanes - DEEP, after, turned(block, -DEEP))
        first_group += lane_groups(len(fields), width)

    high = rows + 2 * DEEP
    edge = jnp.zeros((STEPS, lanes), jnp.float32)
    for n in range(2):
        for t in range(2):
            work[n, t, :STEPS] = edge
            work[n, t, STEPS + high :] = edge
            flux[n, t, :STEPS] = edge

    def sweeps(i, margin):
        half_steps = STEPS // 2
        for begin in (margin, margin + half_steps):
            count = high - 2 * begin
            body = pl.ds(STEPS + begin, count)
            for tile in range(2):
                lon_coef = deep_tiles[2 * half + i, tile, body]
                lat_coef = deep_tiles[3 * half + i, tile, body]
                for member in range(2):
                    field = work[member, tile, body]
                    for step in range(half_steps):
                        if step:
                            work[member, tile, body] = field
                        north = work[member, tile, pl.ds(STEPS + begin + 1, count)]
                        flux_x = lon_coef * (north - field)
                        flux[member, tile, body] = flux_x
                        south = flux[member, tile, pl.ds(STEPS + begin - 1, count)]
                        flux_y = lat_coef * (turned(field, -1) - field)
                        field = (field + (flux_x - south)) + (flux_y - turned(flux_y, 1))
                    work[member, tile, body] = field

    def level(i, carry):
        for tile in range(2):
            body = pl.ds(STEPS, high)
            for member in range(2):
                work[member, tile, body] = deep_tiles[member * half + i, tile, body]
        sweeps(i, 0)
        inner = pl.ds(2 * STEPS, high - 2 * STEPS)
        shallow_rows = pl.ds(STEPS, high - 2 * STEPS)
        center = slice(STEPS, STEPS + rows)
        totals = []
        for tile in range(2):
            gains = [shallow_tiles[m * half + i, tile, shallow_rows] for m in range(2)]
            total = gains[0] * work[0, tile, inner] + gains[1] * work[1, tile, inner]
            totals.append(total[center])
            residual = total - shallow_tiles[2 * half + i, tile, shallow_rows]
            for member in range(2):
                work[member, tile, inner] = gains[member] * residual
        joined = lane < lanes // 2
        total = jnp.where(joined, turned(totals[0], -DEEP), turned(totals[1], DEEP))
        increment[i] = total * keep[5 * half + i]
        sweeps(i, STEPS)
        own = pl.ds(STEPS + DEEP, rows)
        for member, out in enumerate((mine, theirs)):
            parts = [work[member, tile, own] for tile in range(2)]
            out[i] = jnp.where(joined, turned(parts[0], -DEEP), turned(parts[1], DEEP))
        return carry

    lax.fori_loop(0, half, level, 0)


def gradient_kernel(half, vertical, alpha, mine, got, gradient):
    base = lax.axis_index("mem") * half
    other = half - base
    for k in range(2 * half):
        total = alpha[0, k]
        for i in range(half):
            total = total + vertical[base + i, k] * mine[i]
            total = total + vertical[other + i, k] * got[i]
        gradient[0, k] = total


def local(
    alpha_fields, anomalies, lon_faces, lat_faces, normalizer, innovation, misfit_weight, vertical
):
    levels, rows, lanes = lon_faces.shape
    half = levels // 2
    deep_count, shallow_count = 4 * half, 3 * half
    deep_groups = lane_groups(deep_count, DEEP)
    groups = deep_groups + lane_groups(shallow_count, STEPS)
    strip = f32(DEEP * deep_count + STEPS * shallow_count, lanes)
    column = f32(groups, rows, lanes)
    corners = f32(2 * (DEEP * deep_groups + STEPS * (groups - deep_groups)), lanes)
    block = f32(half, rows, lanes)
    high = rows + 2 * DEEP

    inputs = (
        vertical,
        alpha_fields,
        anomalies,
        lon_faces,
        lat_faces,
        normalizer,
        innovation,
        misfit_weight,
    )
    keep, give, alpha = pl.pallas_call(
        functools.partial(prepare_kernel, half),
        out_shape=(f32(6 * half, rows, lanes), f32(levels, rows, lanes), f32(*alpha_fields.shape)),
        in_specs=[HBM] * 8,
        out_specs=(VMEM, VMEM, VMEM),
        scratch_shapes=[
            pltpu.SMEM(vertical.shape, jnp.float32),
            pltpu.VMEM(anomalies.shape, jnp.float32),
            pltpu.VMEM(block.shape, jnp.float32),
            pltpu.VMEM(normalizer.shape, jnp.float32),
            pltpu.VMEM(block.shape, jnp.float32),
            pltpu.VMEM(misfit_weight.shape, jnp.float32),
            pltpu.SemaphoreType.DMA((8,)),
        ],
        compiler_params=PARAMS,
        name="prepare",
    )(*(pltpu.with_memory_space_constraint(value, pltpu.HBM) for value in inputs))
    got = around(give, "mem", 1)

    first, final, west, east = pl.pallas_call(
        functools.partial(pack_kernel, half),
        out_shape=(strip, strip, column, column),
        in_specs=[VMEM] * 2,
        out_specs=(VMEM,) * 4,
        compiler_params=PARAMS,
        name="pack",
    )(keep, got)
    below = around(final, "lon", 1)
    above = around(first, "lon", -1)
    left = around(east, "lat", 1)
    right = around(west, "lat", -1)
    first, final = pl.pallas_call(
        functools.partial(corner_kernel, deep_groups),
        out_shape=(corners, corners),
        in_specs=[VMEM] * 2,
        out_specs=(VMEM,) * 2,
        compiler_params=PARAMS,
        name="corners",
    )(left, right)
    corner_below = around(final, "lon", 1)
    corner_above = around(first, "lon", -1)

    increment, mine, theirs = pl.pallas_call(
        functools.partial(diffuse_kernel, half),
        out_shape=(block, block, block),
        in_specs=[VMEM] * 8,
        out_specs=(VMEM,) * 3,
        scratch_shapes=[
            pltpu.VMEM((deep_count, 2, STEPS + high, lanes), jnp.float32),
            pltpu.VMEM((shallow_count, 2, high, lanes), jnp.float32),
            pltpu.VMEM((2, 2, high + 2 * STEPS, lanes), jnp.float32),
            pltpu.VMEM((2, 2, high + 2 * STEPS, lanes), jnp.float32),
        ],
        compiler_params=PARAMS,
        name="diffuse",
    )(keep, got, below, above, left, right, corner_below, corner_above)
    got = around(theirs, "mem", 1)

    gradient = pl.pallas_call(
        functools.partial(gradient_kernel, half),
        out_shape=f32(*alpha_fields.shape),
        in_specs=[SMEM] + [VMEM] * 3,
        out_specs=VMEM,
        compiler_params=PARAMS,
        name="gradient",
    )(vertical, alpha, mine, got)
    return (increment, gradient)


def solution(mesh):
    return jax.shard_map(
        local,
        mesh=mesh,
        in_specs=(
            P("mem", None, "lon", "lat"),
            P("mem", None, "lon", "lat"),
            P(None, "lon", "lat"),
            P(None, "lon", "lat"),
            P(None, "lon", "lat"),
            P(None, "lon", "lat"),
            P(None, "lon", "lat"),
            P(),
        ),
        out_specs=(P("mem", "lon", "lat"), P("mem", None, "lon", "lat")),
        check_vma=False,
    )
```

```python
import functools
import math

import jax
import jax.numpy as jnp
from jax import lax
from jax.experimental import pallas as pl
from jax.experimental.pallas import tpu as pltpu
from jax.sharding import PartitionSpec as P

STEPS = 8
DEEP = 2 * STEPS
LANES = 128
VMEM = pl.BlockSpec(memory_space=pltpu.VMEM)
SMEM = pl.BlockSpec(memory_space=pltpu.SMEM)
HBM = pl.BlockSpec(memory_space=pltpu.HBM)
PARAMS = pltpu.CompilerParams(vmem_limit_bytes=32 * 1024 * 1024)


def f32(*shape):
    return jax.ShapeDtypeStruct(shape, jnp.float32)


def around(value, axis, steps):
    count = lax.axis_size(axis)
    pairs = [(source, (source + steps) % count) for source in range(count)]
    return lax.ppermute(value, axis, pairs)


def lane_places(deep, shallow):
    places = []
    for width, count in ((DEEP, deep), (STEPS, shallow)):
        for i in range(count):
            group, place = divmod(i * width, LANES)
            if width == STEPS:
                group += -(-deep * DEEP // LANES)
            places.append((width, group, place, (place + 2 * DEEP - width) % LANES))
    return places


def turned(value, shift):
    shift = shift % value.shape[-1]
    return pltpu.roll(value, shift, axis=value.ndim - 1) if shift else value


def mixed(vertical_ref, alpha_ref, level):
    total = vertical_ref[level, 0] * alpha_ref[0, 0]
    for k in range(1, alpha_ref.shape[1]):
        total = total + vertical_ref[level, k] * alpha_ref[0, k]
    return total


def prepare_kernel(
    half,
    vertical_hbm,
    alpha_hbm,
    anomaly_hbm,
    lon_hbm,
    lat_hbm,
    normalizer_hbm,
    innovation_hbm,
    weight_hbm,
    keep,
    give,
    alpha,
    vertical,
    anomaly,
    faces,
    normalizer,
    innovation,
    weight,
    sems,
):
    base = lax.axis_index("mem") * half
    other = half - base
    pairs = [
        (vertical_hbm, vertical),
        (alpha_hbm, alpha),
        (weight_hbm, weight),
        (normalizer_hbm, normalizer),
        (anomaly_hbm, anomaly),
        (innovation_hbm.at[pl.ds(base, half)], innovation),
        (lon_hbm.at[pl.ds(base, half)], keep.at[pl.ds(half, half)]),
        (lat_hbm.at[pl.ds(base, half)], faces),
    ]
    copies = [pltpu.make_async_copy(a, b, sems.at[n]) for n, (a, b) in enumerate(pairs)]
    for copy in copies:
        copy.start()
    copies[0].wait()
    copies[1].wait()
    for i in range(half):
        keep[i] = mixed(vertical, alpha, base + i)
        give[i] = mixed(vertical, alpha, other + i)
    for copy in copies[2:]:
        copy.wait()
    last = lax.axis_index("lat") == lax.axis_size("lat") - 1
    lane = lax.broadcasted_iota(jnp.int32, faces.shape[1:], 1)
    closed = jnp.logical_and(last, lane == faces.shape[2] - 1)
    for i in range(half):
        mine, theirs = base + i, other + i
        root = jnp.sqrt(weight[mine])
        keep[2 * half + i] = jnp.where(closed, 0.0, faces[i])
        keep[3 * half + i] = normalizer[mine] * anomaly[0, mine] * root
        keep[4 * half + i] = root * innovation[i]
        keep[5 * half + i] = 1.0 / root
        give[half + i] = normalizer[theirs] * anomaly[0, theirs] * jnp.sqrt(weight[theirs])


def field_refs(half, keep, got):
    deep = [keep.at[i] for i in range(half)]
    deep += [got.at[i] for i in range(half)]
    deep += [keep.at[half + i] for i in range(2 * half)]
    shallow = [keep.at[3 * half + i] for i in range(half)]
    shallow += [got.at[half + i] for i in range(half)]
    shallow += [keep.at[4 * half + i] for i in range(half)]
    return deep, shallow


def strip_kernel(half, keep, got, first, final):
    deep, shallow = field_refs(half, keep, got)
    rows = keep.shape[1]
    at = 0
    for width, fields in ((DEEP, deep), (STEPS, shallow)):
        for ref in fields:
            first[at : at + width] = ref[:width]
            final[at : at + width] = ref[rows - width :]
            at += width


def in_lanes(lane, place, width):
    if place + width > LANES:
        return jnp.logical_or(lane >= place, lane < place + width - LANES)
    return jnp.logical_and(lane >= place, lane < place + width)


def column_kernel(half, keep, got, below, above, west, east):
    deep, shallow = field_refs(half, keep, got)
    rows, lanes = keep.shape[1:]
    high = rows + 2 * DEEP
    lane = lax.broadcasted_iota(jnp.int32, (1, lanes), 1)
    packs = {}
    at = 0
    for ref, (width, group, place, opposite) in zip(
        deep + shallow, lane_places(len(deep), len(shallow))
    ):
        pieces = (below[at : at + width], ref[...], above[at : at + width])
        at += width
        for n, piece in enumerate(pieces):
            heads, tails = packs.get((group, n), (0.0, 0.0))
            heads = jnp.where(in_lanes(lane, place, width), turned(piece, place), heads)
            tails = jnp.where(in_lanes(lane, opposite, width), turned(piece, place + 2 * DEEP), tails)
            packs[group, n] = heads, tails
    at = 0
    for heads, tails in packs.values():
        count = heads.shape[0]
        west[at : at + count] = heads
        east[at : at + count] = tails
        at += count


def diffusion(half, field_tiles, other_tiles, face_tiles, shallow_tiles, totals):
    high = field_tiles.shape[1] - 2 * STEPS
    rows = high - 2 * DEEP
    edge = jnp.zeros((STEPS, field_tiles.shape[2]), jnp.float32)
    for n in range(2 * half):
        face_tiles[n, :STEPS] = edge
        for ref in (field_tiles, other_tiles):
            ref[n, :STEPS] = edge
            ref[n, STEPS + high :] = edge

    def step(source, target, begin, count):
        body = pl.ds(STEPS + begin, count)
        up = pl.ds(STEPS + begin + 1, count)
        down = pl.ds(STEPS + begin - 1, count)
        for i in range(half):
            lon_coef = face_tiles[i, body]
            lon_before = face_tiles[i, down]
            lat_coef = face_tiles[half + i, body]
            for n in (i, half + i):
                field = source[n, body]
                flux_x = lon_coef * (source[n, up] - field)
                flux_x = flux_x - lon_before * (field - source[n, down])
                flux_y = lat_coef * (turned(field, -1) - field)
                target[n, body] = (field + flux_x) + (flux_y - turned(flux_y, 1))

    def root(margin):
        for begin in (margin, margin + STEPS // 2):
            count = high - 2 * begin

            def pair(_, carry):
                step(field_tiles, other_tiles, begin, count)
                step(other_tiles, field_tiles, begin, count)
                return carry

            lax.fori_loop(0, STEPS // 4, pair, 0)

    root(0)
    inner = pl.ds(2 * STEPS, rows + 2 * STEPS)
    for i in range(half):
        gains = [shallow_tiles[m * half + i] for m in range(2)]
        total = sum(gains[m] * field_tiles[m * half + i, inner] for m in range(2))
        totals[i] = total[STEPS : STEPS + rows]
        residual = total - shallow_tiles[2 * half + i]
        for m in range(2):
            field_tiles[m * half + i, inner] = gains[m] * residual
    root(STEPS)


def tile_targets(half, field_tiles, face_tiles, shallow_tiles):
    high = field_tiles.shape[1] - 2 * STEPS
    targets = [field_tiles.at[n, pl.ds(STEPS, high)] for n in range(2 * half)]
    targets += [face_tiles.at[n, pl.ds(STEPS, high)] for n in range(2 * half)]
    return targets + [shallow_tiles.at[n] for n in range(3 * half)]


def main_kernel(half, keep, got, below, above, total, mine, theirs, *tiles):
    field_tiles, other_tiles, face_tiles, shallow_tiles = tiles
    deep, shallow = field_refs(half, keep, got)
    rows = keep.shape[1]
    at = 0
    for n, (ref, out) in enumerate(
        zip(deep + shallow, tile_targets(half, field_tiles, face_tiles, shallow_tiles))
    ):
        width = DEEP if n < len(deep) else STEPS
        out[:width] = below[at : at + width]
        out[width : width + rows] = ref[...]
        out[width + rows :] = above[at : at + width]
        at += width
    diffusion(half, *tiles, total)
    own = pl.ds(STEPS + DEEP, rows)
    for i in range(half):
        mine[i] = field_tiles[i, own]
        theirs[i] = field_tiles[half + i, own]


def edge_kernel(
    half,
    keep,
    got,
    below,
    above,
    left,
    right,
    main_total,
    main_mine,
    main_theirs,
    increment,
    mine,
    theirs,
    *tiles,
):
    field_tiles, other_tiles, face_tiles, shallow_tiles, totals = tiles
    deep, shallow = field_refs(half, keep, got)
    rows, lanes = keep.shape[1:]
    lane = lax.broadcasted_iota(jnp.int32, (1, lanes), 1)
    at = 0
    group_rows = {DEEP: rows + 2 * DEEP, STEPS: rows + 2 * STEPS}
    for ref, out, (width, group, place, _) in zip(
        deep + shallow,
        tile_targets(half, field_tiles, face_tiles, shallow_tiles),
        lane_places(len(deep), len(shallow)),
    ):
        pieces = (below[at : at + width], ref[...], above[at : at + width])
        at += width
        start = group * group_rows[DEEP]
        offset = 0
        for piece in pieces:
            count = piece.shape[0]
            here = pl.ds(start + offset, count)
            sides = jnp.where(in_lanes(lane, place, width), right[here], left[here])
            own = jnp.where(lane < lanes - 3 * DEEP, turned(piece, 2 * DEEP), piece)
            out[offset : offset + count] = jnp.where(lane < 2 * DEEP, turned(sides, -place), own)
            offset += count
    diffusion(half, field_tiles, other_tiles, face_tiles, shallow_tiles, totals)
    body = pl.ds(STEPS + DEEP, rows)

    def joined(main, sides):
        sides = jnp.where(lane < DEEP, turned(sides, -2 * DEEP), sides)
        return jnp.where(in_lanes(lane, DEEP, lanes - 2 * DEEP), main, sides)

    for i in range(half):
        increment[i] = joined(main_total[i], totals[i]) * keep[5 * half + i]
        mine[i] = joined(main_mine[i], field_tiles[i, body])
        theirs[i] = joined(main_theirs[i], field_tiles[half + i, body])


def gradient_kernel(half, vertical, alpha, mine, got, gradient):
    base = lax.axis_index("mem") * half
    other = half - base
    for k in range(2 * half):
        total = alpha[0, k]
        for i in range(half):
            total = total + vertical[base + i, k] * mine[i]
            total = total + vertical[other + i, k] * got[i]
        gradient[0, k] = total


def local(
    alpha_fields, anomalies, lon_faces, lat_faces, normalizer, innovation, misfit_weight, vertical
):
    levels, rows, lanes = lon_faces.shape
    half = levels // 2
    high = rows + 2 * DEEP
    strip = f32(DEEP * 4 * half + STEPS * 3 * half, lanes)
    deep_groups = -(-4 * half * DEEP // lanes)
    shallow_groups = -(-3 * half * STEPS // lanes)
    column = f32(deep_groups * high + shallow_groups * (rows + 2 * STEPS), lanes)
    block = f32(half, rows, lanes)
    tiles = [
        pltpu.VMEM((levels, high + 2 * STEPS, lanes), jnp.float32),
        pltpu.VMEM((levels, high + 2 * STEPS, lanes), jnp.float32),
        pltpu.VMEM((levels, high + STEPS, lanes), jnp.float32),
        pltpu.VMEM((3 * half, rows + 2 * STEPS, lanes), jnp.float32),
    ]

    inputs = (
        vertical,
        alpha_fields,
        anomalies,
        lon_faces,
        lat_faces,
        normalizer,
        innovation,
        misfit_weight,
    )
    keep, give, alpha = pl.pallas_call(
        functools.partial(prepare_kernel, half),
        out_shape=(f32(6 * half, rows, lanes), f32(levels, rows, lanes), f32(*alpha_fields.shape)),
        in_specs=[HBM] * 8,
        out_specs=(VMEM, VMEM, VMEM),
        scratch_shapes=[
            pltpu.SMEM(vertical.shape, jnp.float32),
            pltpu.VMEM(anomalies.shape, jnp.float32),
            pltpu.VMEM(block.shape, jnp.float32),
            pltpu.VMEM(normalizer.shape, jnp.float32),
            pltpu.VMEM(block.shape, jnp.float32),
            pltpu.VMEM(misfit_weight.shape, jnp.float32),
            pltpu.SemaphoreType.DMA((8,)),
        ],
        compiler_params=PARAMS,
        name="prepare",
    )(*(pltpu.with_memory_space_constraint(value, pltpu.HBM) for value in inputs))
    got = around(give, "mem", 1)

    first, final = pl.pallas_call(
        functools.partial(strip_kernel, half),
        out_shape=(strip, strip),
        in_specs=[VMEM] * 2,
        out_specs=(VMEM,) * 2,
        compiler_params=PARAMS,
        name="strips",
    )(keep, got)
    below = around(final, "lon", 1)
    above = around(first, "lon", -1)
    west, east = pl.pallas_call(
        functools.partial(column_kernel, half),
        out_shape=(column, column),
        in_specs=[VMEM] * 4,
        out_specs=(VMEM,) * 2,
        compiler_params=PARAMS,
        name="columns",
    )(keep, got, below, above)
    left = around(east, "lat", 1)
    right = around(west, "lat", -1)
    main = pl.pallas_call(
        functools.partial(main_kernel, half),
        out_shape=(block, block, block),
        in_specs=[VMEM] * 4,
        out_specs=(VMEM,) * 3,
        scratch_shapes=tiles,
        compiler_params=PARAMS,
        name="main",
    )(keep, got, below, above)
    increment, mine, theirs = pl.pallas_call(
        functools.partial(edge_kernel, half),
        out_shape=(block, block, block),
        in_specs=[VMEM] * 9,
        out_specs=(VMEM,) * 3,
        scratch_shapes=tiles + [pltpu.VMEM(block.shape, jnp.float32)],
        compiler_params=PARAMS,
        name="edge",
    )(keep, got, below, above, left, right, *main)
    got = around(theirs, "mem", 1)

    gradient = pl.pallas_call(
        functools.partial(gradient_kernel, half),
        out_shape=f32(*alpha_fields.shape),
        in_specs=[SMEM] + [VMEM] * 3,
        out_specs=VMEM,
        compiler_params=PARAMS,
        name="gradient",
    )(vertical, alpha, mine, got)
    return (increment, gradient)


def solution(mesh):
    return jax.shard_map(
        local,
        mesh=mesh,
        in_specs=(
            P("mem", None, "lon", "lat"),
            P("mem", None, "lon", "lat"),
            P(None, "lon", "lat"),
            P(None, "lon", "lat"),
            P(None, "lon", "lat"),
            P(None, "lon", "lat"),
            P(None, "lon", "lat"),
            P(),
        ),
        out_specs=(P("mem", "lon", "lat"), P("mem", None, "lon", "lat")),
        check_vma=False,
    )
```

```python
import functools
import math

import jax
import jax.numpy as jnp
from jax import lax
from jax.experimental import pallas as pl
from jax.experimental.pallas import tpu as pltpu
from jax.sharding import PartitionSpec as P

STEPS = 8
DEEP = 2 * STEPS
LANES = 128
VMEM = pl.BlockSpec(memory_space=pltpu.VMEM)
SMEM = pl.BlockSpec(memory_space=pltpu.SMEM)
HBM = pl.BlockSpec(memory_space=pltpu.HBM)
PARAMS = pltpu.CompilerParams(vmem_limit_bytes=32 * 1024 * 1024)


def f32(*shape):
    return jax.ShapeDtypeStruct(shape, jnp.float32)


def around(value, axis, steps):
    count = lax.axis_size(axis)
    pairs = [(source, (source + steps) % count) for source in range(count)]
    return lax.ppermute(value, axis, pairs)


def lane_places(deep, shallow):
    places = []
    for width, count in ((DEEP, deep), (STEPS, shallow)):
        for i in range(count):
            group, place = divmod(i * width, LANES)
            if width == STEPS:
                group += -(-deep * DEEP // LANES)
            places.append((width, group, place, (place + 2 * DEEP - width) % LANES))
    return places


def turned(value, shift):
    shift = shift % value.shape[-1]
    return pltpu.roll(value, shift, axis=value.ndim - 1) if shift else value


def mixed(vertical_ref, alpha_ref, level):
    total = vertical_ref[level, 0] * alpha_ref[0, 0]
    for k in range(1, alpha_ref.shape[1]):
        total = total + vertical_ref[level, k] * alpha_ref[0, k]
    return total


def prepare_kernel(
    half,
    vertical_hbm,
    alpha_hbm,
    anomaly_hbm,
    lon_hbm,
    lat_hbm,
    normalizer_hbm,
    innovation_hbm,
    weight_hbm,
    keep,
    give,
    alpha,
    vertical,
    anomaly,
    faces,
    normalizer,
    innovation,
    weight,
    sems,
):
    base = lax.axis_index("mem") * half
    other = half - base
    pairs = [
        (vertical_hbm, vertical),
        (alpha_hbm, alpha),
        (weight_hbm, weight),
        (normalizer_hbm, normalizer),
        (anomaly_hbm, anomaly),
        (innovation_hbm.at[pl.ds(base, half)], innovation),
        (lon_hbm.at[pl.ds(base, half)], keep.at[pl.ds(half, half)]),
        (lat_hbm.at[pl.ds(base, half)], faces),
    ]
    copies = [pltpu.make_async_copy(a, b, sems.at[n]) for n, (a, b) in enumerate(pairs)]
    for copy in copies:
        copy.start()
    copies[0].wait()
    copies[1].wait()
    for i in range(half):
        keep[i] = mixed(vertical, alpha, base + i)
        give[i] = mixed(vertical, alpha, other + i)
    for copy in copies[2:]:
        copy.wait()
    last = lax.axis_index("lat") == lax.axis_size("lat") - 1
    lane = lax.broadcasted_iota(jnp.int32, faces.shape[1:], 1)
    closed = jnp.logical_and(last, lane == faces.shape[2] - 1)
    for i in range(half):
        mine, theirs = base + i, other + i
        root = jnp.sqrt(weight[mine])
        keep[2 * half + i] = jnp.where(closed, 0.0, faces[i])
        keep[3 * half + i] = normalizer[mine] * anomaly[0, mine] * root
        keep[4 * half + i] = root * innovation[i]
        keep[5 * half + i] = 1.0 / root
        give[half + i] = normalizer[theirs] * anomaly[0, theirs] * jnp.sqrt(weight[theirs])


def field_refs(half, keep, got):
    deep = [keep.at[i] for i in range(half)]
    deep += [got.at[i] for i in range(half)]
    deep += [keep.at[half + i] for i in range(2 * half)]
    shallow = [keep.at[3 * half + i] for i in range(half)]
    shallow += [got.at[half + i] for i in range(half)]
    shallow += [keep.at[4 * half + i] for i in range(half)]
    return deep, shallow


def strip_kernel(half, keep, got, first, final):
    deep, shallow = field_refs(half, keep, got)
    rows = keep.shape[1]
    at = 0
    for width, fields in ((DEEP, deep), (STEPS, shallow)):
        for ref in fields:
            first[at : at + width] = ref[:width]
            final[at : at + width] = ref[rows - width :]
            at += width


def in_lanes(lane, place, width):
    if place + width > LANES:
        return jnp.logical_or(lane >= place, lane < place + width - LANES)
    return jnp.logical_and(lane >= place, lane < place + width)


def column_kernel(half, keep, got, below, above, west, east):
    deep, shallow = field_refs(half, keep, got)
    rows, lanes = keep.shape[1:]
    high = rows + 2 * DEEP
    lane = lax.broadcasted_iota(jnp.int32, (1, lanes), 1)
    packs = {}
    at = 0
    for ref, (width, group, place, opposite) in zip(
        deep + shallow, lane_places(len(deep), len(shallow))
    ):
        pieces = (below[at : at + width], ref[...], above[at : at + width])
        at += width
        for n, piece in enumerate(pieces):
            heads, tails = packs.get((group, n), (0.0, 0.0))
            heads = jnp.where(in_lanes(lane, place, width), turned(piece, place), heads)
            tails = jnp.where(in_lanes(lane, opposite, width), turned(piece, place + 2 * DEEP), tails)
            packs[group, n] = heads, tails
    at = 0
    for heads, tails in packs.values():
        count = heads.shape[0]
        west[at : at + count] = heads
        east[at : at + count] = tails
        at += count


def diffusion(half, field_tiles, other_tiles, face_tiles, shallow_tiles, totals):
    high = field_tiles.shape[1] - 2 * STEPS
    rows = high - 2 * DEEP
    edge = jnp.zeros((STEPS, field_tiles.shape[2]), jnp.float32)
    for n in range(2 * half):
        face_tiles[n, :STEPS] = edge
        for ref in (field_tiles, other_tiles):
            ref[n, :STEPS] = edge
            ref[n, STEPS + high :] = edge

    zero = lax.axis_index("mem") // 2

    def step(source, target, begin, count):
        begin = begin + zero
        body = pl.ds(STEPS + begin, count)
        up = pl.ds(STEPS + begin + 1, count)
        down = pl.ds(STEPS + begin - 1, count)
        for i in range(half):
            lon_coef = face_tiles[i, body]
            lon_before = face_tiles[i, down]
            lat_coef = face_tiles[half + i, body]
            for n in (i, half + i):
                field = source[n, body]
                flux_x = lon_coef * (source[n, up] - field)
                flux_x = flux_x - lon_before * (field - source[n, down])
                flux_y = lat_coef * (turned(field, -1) - field)
                target[n, body] = (field + flux_x) + (flux_y - turned(flux_y, 1))

    def root(margin):
        for begin in (margin, margin + STEPS // 2):
            count = high - 2 * begin

            def pair(_, carry):
                step(field_tiles, other_tiles, begin, count)
                step(other_tiles, field_tiles, begin, count)
                return carry

            lax.fori_loop(0, STEPS // 4, pair, 0)

    root(0)
    inner = pl.ds(2 * STEPS, rows + 2 * STEPS)
    for i in range(half):
        gains = [shallow_tiles[m * half + i] for m in range(2)]
        total = sum(gains[m] * field_tiles[m * half + i, inner] for m in range(2))
        totals[i] = total[STEPS : STEPS + rows]
        residual = total - shallow_tiles[2 * half + i]
        for m in range(2):
            field_tiles[m * half + i, inner] = gains[m] * residual
    root(STEPS)


def tile_targets(half, field_tiles, face_tiles, shallow_tiles):
    high = field_tiles.shape[1] - 2 * STEPS
    targets = [field_tiles.at[n, pl.ds(STEPS, high)] for n in range(2 * half)]
    targets += [face_tiles.at[n, pl.ds(STEPS, high)] for n in range(2 * half)]
    return targets + [shallow_tiles.at[n] for n in range(3 * half)]


def main_kernel(half, keep, got, below, above, total, mine, theirs, edge_own, *tiles):
    field_tiles, other_tiles, face_tiles, shallow_tiles = tiles
    deep, shallow = field_refs(half, keep, got)
    rows, lanes = keep.shape[1:]
    lane = lax.broadcasted_iota(jnp.int32, (1, lanes), 1)
    at = 0
    edge_at = 0
    for n, (ref, out) in enumerate(
        zip(deep + shallow, tile_targets(half, field_tiles, face_tiles, shallow_tiles))
    ):
        width = DEEP if n < len(deep) else STEPS
        offset = 0
        for piece in (below[at : at + width], ref[...], above[at : at + width]):
            count = piece.shape[0]
            out[offset : offset + count] = piece
            own = jnp.where(lane < lanes - 3 * DEEP, turned(piece, 2 * DEEP), piece)
            edge_own[edge_at : edge_at + count] = own
            offset += count
            edge_at += count
        at += width
    diffusion(half, *tiles, total)
    own = pl.ds(STEPS + DEEP, rows)
    for i in range(half):
        mine[i] = field_tiles[i, own]
        theirs[i] = field_tiles[half + i, own]


def edge_kernel(
    half,
    keep,
    left,
    right,
    main_total,
    main_mine,
    main_theirs,
    edge_own,
    increment,
    mine,
    theirs,
    *tiles,
):
    field_tiles, other_tiles, face_tiles, shallow_tiles, totals = tiles
    rows, lanes = keep.shape[1:]
    lane = lax.broadcasted_iota(jnp.int32, (1, lanes), 1)
    high = rows + 2 * DEEP
    at = 0
    for out, (width, group, place, _) in zip(
        tile_targets(half, field_tiles, face_tiles, shallow_tiles),
        lane_places(4 * half, 3 * half),
    ):
        count = rows + 2 * width
        here = pl.ds(group * high, count)
        sides = jnp.where(in_lanes(lane, place, width), right[here], left[here])
        out[...] = jnp.where(lane < 2 * DEEP, turned(sides, -place), edge_own[at : at + count])
        at += count
    diffusion(half, field_tiles, other_tiles, face_tiles, shallow_tiles, totals)
    body = pl.ds(STEPS + DEEP, rows)

    def joined(main, sides):
        sides = jnp.where(lane < DEEP, turned(sides, -2 * DEEP), sides)
        return jnp.where(in_lanes(lane, DEEP, lanes - 2 * DEEP), main, sides)

    for i in range(half):
        increment[i] = joined(main_total[i], totals[i]) * keep[5 * half + i]
        mine[i] = joined(main_mine[i], field_tiles[i, body])
        theirs[i] = joined(main_theirs[i], field_tiles[half + i, body])


def partial_kernel(half, vertical, alpha, mine, partial, splat):
    base = lax.axis_index("mem") * half
    other = half - base
    for k in range(2 * half):
        total = alpha[0, k]
        for i in range(half):
            total = total + vertical[base + i, k] * mine[i]
            splat[i, k : k + 1] = jnp.full((1, splat.shape[2]), vertical[other + i, k])
        partial[k] = total


def gradient_kernel(half, partial, splat, got, gradient):
    for k in range(2 * half):
        total = partial[k]
        for i in range(half):
            total = total + splat[i, k : k + 1] * got[i]
        gradient[0, k] = total


def local(
    alpha_fields, anomalies, lon_faces, lat_faces, normalizer, innovation, misfit_weight, vertical
):
    levels, rows, lanes = lon_faces.shape
    half = levels // 2
    high = rows + 2 * DEEP
    strip = f32(DEEP * 4 * half + STEPS * 3 * half, lanes)
    deep_groups = -(-4 * half * DEEP // lanes)
    shallow_groups = -(-3 * half * STEPS // lanes)
    column = f32(deep_groups * high + shallow_groups * (rows + 2 * STEPS), lanes)
    block = f32(half, rows, lanes)
    tiles = [
        pltpu.VMEM((levels, high + 2 * STEPS, lanes), jnp.float32),
        pltpu.VMEM((levels, high + 2 * STEPS, lanes), jnp.float32),
        pltpu.VMEM((levels, high + STEPS, lanes), jnp.float32),
        pltpu.VMEM((3 * half, rows + 2 * STEPS, lanes), jnp.float32),
    ]

    inputs = (
        vertical,
        alpha_fields,
        anomalies,
        lon_faces,
        lat_faces,
        normalizer,
        innovation,
        misfit_weight,
    )
    keep, give, alpha = pl.pallas_call(
        functools.partial(prepare_kernel, half),
        out_shape=(f32(6 * half, rows, lanes), f32(levels, rows, lanes), f32(*alpha_fields.shape)),
        in_specs=[HBM] * 8,
        out_specs=(VMEM, VMEM, VMEM),
        scratch_shapes=[
            pltpu.SMEM(vertical.shape, jnp.float32),
            pltpu.VMEM(anomalies.shape, jnp.float32),
            pltpu.VMEM(block.shape, jnp.float32),
            pltpu.VMEM(normalizer.shape, jnp.float32),
            pltpu.VMEM(block.shape, jnp.float32),
            pltpu.VMEM(misfit_weight.shape, jnp.float32),
            pltpu.SemaphoreType.DMA((8,)),
        ],
        compiler_params=PARAMS,
        name="prepare",
    )(*(pltpu.with_memory_space_constraint(value, pltpu.HBM) for value in inputs))
    got = around(give, "mem", 1)

    first, final = pl.pallas_call(
        functools.partial(strip_kernel, half),
        out_shape=(strip, strip),
        in_specs=[VMEM] * 2,
        out_specs=(VMEM,) * 2,
        compiler_params=PARAMS,
        name="strips",
    )(keep, got)
    below = around(final, "lon", 1)
    above = around(first, "lon", -1)
    west, east = pl.pallas_call(
        functools.partial(column_kernel, half),
        out_shape=(column, column),
        in_specs=[VMEM] * 4,
        out_specs=(VMEM,) * 2,
        compiler_params=PARAMS,
        name="columns",
    )(keep, got, below, above)
    left = around(east, "lat", 1)
    right = around(west, "lat", -1)
    edge_own = f32(high * 4 * half + (rows + 2 * STEPS) * 3 * half, lanes)
    main = pl.pallas_call(
        functools.partial(main_kernel, half),
        out_shape=(block, block, block, edge_own),
        in_specs=[VMEM] * 4,
        out_specs=(VMEM,) * 4,
        scratch_shapes=tiles,
        compiler_params=PARAMS,
        name="main",
    )(keep, got, below, above)
    increment, mine, theirs = pl.pallas_call(
        functools.partial(edge_kernel, half),
        out_shape=(block, block, block),
        in_specs=[VMEM] * 7,
        out_specs=(VMEM,) * 3,
        scratch_shapes=tiles + [pltpu.VMEM(block.shape, jnp.float32)],
        compiler_params=PARAMS,
        name="edge",
    )(keep, left, right, *main)
    got = around(theirs, "mem", 1)

    partial, splat = pl.pallas_call(
        functools.partial(partial_kernel, half),
        out_shape=(f32(levels, rows, lanes), f32(half, levels, lanes)),
        in_specs=[SMEM] + [VMEM] * 2,
        out_specs=(VMEM, VMEM),
        compiler_params=PARAMS,
        name="partial",
    )(vertical, alpha, mine)
    gradient = pl.pallas_call(
        functools.partial(gradient_kernel, half),
        out_shape=f32(*alpha_fields.shape),
        in_specs=[VMEM] * 3,
        out_specs=VMEM,
        compiler_params=PARAMS,
        name="gradient",
    )(partial, splat, got)
    return (increment, gradient)


def solution(mesh):
    return jax.shard_map(
        local,
        mesh=mesh,
        in_specs=(
            P("mem", None, "lon", "lat"),
            P("mem", None, "lon", "lat"),
            P(None, "lon", "lat"),
            P(None, "lon", "lat"),
            P(None, "lon", "lat"),
            P(None, "lon", "lat"),
            P(None, "lon", "lat"),
            P(),
        ),
        out_specs=(P("mem", "lon", "lat"), P("mem", None, "lon", "lat")),
        check_vma=False,
    )
```

```python
import functools
import math

import jax
import jax.numpy as jnp
from jax import lax
from jax.experimental import pallas as pl
from jax.experimental.pallas import tpu as pltpu
from jax.sharding import PartitionSpec as P

STEPS = 8
DEEP = 2 * STEPS
LANES = 128
TILE = 8
VMEM = pl.BlockSpec(memory_space=pltpu.VMEM)
SMEM = pl.BlockSpec(memory_space=pltpu.SMEM)
HBM = pl.BlockSpec(memory_space=pltpu.HBM)
PARAMS = pltpu.CompilerParams(vmem_limit_bytes=32 * 1024 * 1024)


def f32(*shape):
    return jax.ShapeDtypeStruct(shape, jnp.float32)


def around(value, axis, steps):
    count = lax.axis_size(axis)
    pairs = [(source, (source + steps) % count) for source in range(count)]
    return lax.ppermute(value, axis, pairs)


def lane_places(deep, shallow):
    places = []
    for width, count in ((DEEP, deep), (STEPS, shallow)):
        for i in range(count):
            group, place = divmod(i * width, LANES)
            if width == STEPS:
                group += -(-deep * DEEP // LANES)
            places.append((width, group, place, (place + 2 * DEEP - width) % LANES))
    return places


def turned(value, shift):
    shift = shift % value.shape[-1]
    return pltpu.roll(value, shift, axis=value.ndim - 1) if shift else value


def mixed(vertical_ref, alpha_ref, level):
    total = vertical_ref[level, 0] * alpha_ref[0, 0]
    for k in range(1, alpha_ref.shape[1]):
        total = total + vertical_ref[level, k] * alpha_ref[0, k]
    return total


def prepare_kernel(
    half,
    vertical_hbm,
    alpha_hbm,
    anomaly_hbm,
    lon_hbm,
    lat_hbm,
    normalizer_hbm,
    innovation_hbm,
    weight_hbm,
    keep,
    give,
    alpha,
    vertical,
    anomaly,
    faces,
    normalizer,
    innovation,
    weight,
    sems,
):
    base = lax.axis_index("mem") * half
    other = half - base
    pairs = [
        (vertical_hbm, vertical),
        (alpha_hbm, alpha),
        (weight_hbm, weight),
        (normalizer_hbm, normalizer),
        (anomaly_hbm, anomaly),
        (innovation_hbm.at[pl.ds(base, half)], innovation),
        (lon_hbm.at[pl.ds(base, half)], keep.at[pl.ds(half, half)]),
        (lat_hbm.at[pl.ds(base, half)], faces),
    ]
    copies = [pltpu.make_async_copy(a, b, sems.at[n]) for n, (a, b) in enumerate(pairs)]
    for copy in copies:
        copy.start()
    copies[0].wait()
    copies[1].wait()
    for i in range(half):
        keep[i] = mixed(vertical, alpha, base + i)
        give[i] = mixed(vertical, alpha, other + i)
    for copy in copies[2:]:
        copy.wait()
    last = lax.axis_index("lat") == lax.axis_size("lat") - 1
    lane = lax.broadcasted_iota(jnp.int32, faces.shape[1:], 1)
    closed = jnp.logical_and(last, lane == faces.shape[2] - 1)
    for i in range(half):
        mine, theirs = base + i, other + i
        root = jnp.sqrt(weight[mine])
        keep[2 * half + i] = jnp.where(closed, 0.0, faces[i])
        keep[3 * half + i] = normalizer[mine] * anomaly[0, mine] * root
        keep[4 * half + i] = root * innovation[i]
        keep[5 * half + i] = 1.0 / root
        give[half + i] = normalizer[theirs] * anomaly[0, theirs] * jnp.sqrt(weight[theirs])


def field_refs(half, keep, got):
    deep = [keep.at[i] for i in range(half)]
    deep += [got.at[i] for i in range(half)]
    deep += [keep.at[half + i] for i in range(2 * half)]
    shallow = [keep.at[3 * half + i] for i in range(half)]
    shallow += [got.at[half + i] for i in range(half)]
    shallow += [keep.at[4 * half + i] for i in range(half)]
    return deep, shallow


def strip_kernel(half, keep, got, first, final):
    deep, shallow = field_refs(half, keep, got)
    rows = keep.shape[1]
    at = 0
    for width, fields in ((DEEP, deep), (STEPS, shallow)):
        for ref in fields:
            first[at : at + width] = ref[:width]
            final[at : at + width] = ref[rows - width :]
            at += width


def in_lanes(lane, place, width):
    if place + width > LANES:
        return jnp.logical_or(lane >= place, lane < place + width - LANES)
    return jnp.logical_and(lane >= place, lane < place + width)


def column_kernel(half, keep, got, below, above, west, east):
    deep, shallow = field_refs(half, keep, got)
    rows, lanes = keep.shape[1:]
    high = rows + 2 * DEEP
    lane = lax.broadcasted_iota(jnp.int32, (1, lanes), 1)
    packs = {}
    at = 0
    for ref, (width, group, place, opposite) in zip(
        deep + shallow, lane_places(len(deep), len(shallow))
    ):
        pieces = (below[at : at + width], ref[...], above[at : at + width])
        at += width
        for n, piece in enumerate(pieces):
            heads, tails = packs.get((group, n), (0.0, 0.0))
            heads = jnp.where(in_lanes(lane, place, width), turned(piece, place), heads)
            tails = jnp.where(in_lanes(lane, opposite, width), turned(piece, place + 2 * DEEP), tails)
            packs[group, n] = heads, tails
    at = 0
    for heads, tails in packs.values():
        count = heads.shape[0]
        west[at : at + count] = heads
        east[at : at + count] = tails
        at += count


def diffusion(half, field_tiles, other_tiles, face_tiles, shallow_tiles, totals):
    high = field_tiles.shape[1] - 2 * STEPS
    rows = high - 2 * DEEP
    edge = jnp.zeros((STEPS, field_tiles.shape[2]), jnp.float32)
    for n in range(2 * half):
        face_tiles[n, :STEPS] = edge
        for ref in (field_tiles, other_tiles):
            ref[n, :STEPS] = edge
            ref[n, STEPS + high :] = edge

    zero = lax.axis_index("mem") // 2

    def step(source, target, begin, end):
        for i in range(half):
            for at in range(begin, end, TILE):
                here = pl.ds(at, TILE)
                up = pl.ds(at + 1 + zero, TILE)
                down = pl.ds(at - 1 + zero, TILE)
                lon_coef = face_tiles[i, here]
                lon_before = face_tiles[i, down]
                lat_coef = face_tiles[half + i, here]
                for n in (i, half + i):
                    field = source[n, here]
                    flux_x = lon_coef * (source[n, up] - field)
                    flux_x = flux_x - lon_before * (field - source[n, down])
                    flux_y = lat_coef * (turned(field, -1) - field)
                    target[n, here] = (field + flux_x) + (flux_y - turned(flux_y, 1))

    def root(margin):
        begin, end = STEPS + margin, STEPS + high - margin

        def pair(_, carry):
            step(field_tiles, other_tiles, begin, end)
            step(other_tiles, field_tiles, begin, end)
            return carry

        lax.fori_loop(0, STEPS // 2, pair, 0)

    root(0)
    inner = pl.ds(2 * STEPS, rows + 2 * STEPS)
    for i in range(half):
        gains = [shallow_tiles[m * half + i] for m in range(2)]
        total = sum(gains[m] * field_tiles[m * half + i, inner] for m in range(2))
        totals[i] = total[STEPS : STEPS + rows]
        residual = total - shallow_tiles[2 * half + i]
        for m in range(2):
            field_tiles[m * half + i, inner] = gains[m] * residual
    root(STEPS)


def tile_targets(half, field_tiles, face_tiles, shallow_tiles):
    high = field_tiles.shape[1] - 2 * STEPS
    targets = [field_tiles.at[n, pl.ds(STEPS, high)] for n in range(2 * half)]
    targets += [face_tiles.at[n, pl.ds(STEPS, high)] for n in range(2 * half)]
    return targets + [shallow_tiles.at[n] for n in range(3 * half)]


def main_kernel(half, keep, got, below, above, total, mine, theirs, edge_own, *tiles):
    field_tiles, other_tiles, face_tiles, shallow_tiles = tiles
    deep, shallow = field_refs(half, keep, got)
    rows, lanes = keep.shape[1:]
    lane = lax.broadcasted_iota(jnp.int32, (1, lanes), 1)
    at = 0
    edge_at = 0
    for n, (ref, out) in enumerate(
        zip(deep + shallow, tile_targets(half, field_tiles, face_tiles, shallow_tiles))
    ):
        width = DEEP if n < len(deep) else STEPS
        offset = 0
        for piece in (below[at : at + width], ref[...], above[at : at + width]):
            count = piece.shape[0]
            out[offset : offset + count] = piece
            own = jnp.where(lane < lanes - 3 * DEEP, turned(piece, 2 * DEEP), piece)
            edge_own[edge_at : edge_at + count] = own
            offset += count
            edge_at += count
        at += width
    diffusion(half, *tiles, total)
    own = pl.ds(STEPS + DEEP, rows)
    for i in range(half):
        mine[i] = field_tiles[i, own]
        theirs[i] = field_tiles[half + i, own]


def edge_kernel(
    half,
    keep,
    left,
    right,
    main_total,
    main_mine,
    main_theirs,
    edge_own,
    increment,
    mine,
    theirs,
    *tiles,
):
    field_tiles, other_tiles, face_tiles, shallow_tiles, totals = tiles
    rows, lanes = keep.shape[1:]
    lane = lax.broadcasted_iota(jnp.int32, (1, lanes), 1)
    high = rows + 2 * DEEP
    at = 0
    for out, (width, group, place, _) in zip(
        tile_targets(half, field_tiles, face_tiles, shallow_tiles),
        lane_places(4 * half, 3 * half),
    ):
        count = rows + 2 * width
        here = pl.ds(group * high, count)
        sides = jnp.where(in_lanes(lane, place, width), right[here], left[here])
        out[...] = jnp.where(lane < 2 * DEEP, turned(sides, -place), edge_own[at : at + count])
        at += count
    diffusion(half, field_tiles, other_tiles, face_tiles, shallow_tiles, totals)
    body = pl.ds(STEPS + DEEP, rows)

    def joined(main, sides):
        sides = jnp.where(lane < DEEP, turned(sides, -2 * DEEP), sides)
        return jnp.where(in_lanes(lane, DEEP, lanes - 2 * DEEP), main, sides)

    for i in range(half):
        increment[i] = joined(main_total[i], totals[i]) * keep[5 * half + i]
        mine[i] = joined(main_mine[i], field_tiles[i, body])
        theirs[i] = joined(main_theirs[i], field_tiles[half + i, body])


def partial_kernel(half, vertical, alpha, mine, partial, splat):
    base = lax.axis_index("mem") * half
    other = half - base
    for k in range(2 * half):
        total = alpha[0, k]
        for i in range(half):
            total = total + vertical[base + i, k] * mine[i]
            splat[i, k : k + 1] = jnp.full((1, splat.shape[2]), vertical[other + i, k])
        partial[k] = total


def gradient_kernel(half, partial, splat, got, gradient):
    for k in range(2 * half):
        total = partial[k]
        for i in range(half):
            total = total + splat[i, k : k + 1] * got[i]
        gradient[0, k] = total


def local(
    alpha_fields, anomalies, lon_faces, lat_faces, normalizer, innovation, misfit_weight, vertical
):
    levels, rows, lanes = lon_faces.shape
    half = levels // 2
    high = rows + 2 * DEEP
    strip = f32(DEEP * 4 * half + STEPS * 3 * half, lanes)
    deep_groups = -(-4 * half * DEEP // lanes)
    shallow_groups = -(-3 * half * STEPS // lanes)
    column = f32(deep_groups * high + shallow_groups * (rows + 2 * STEPS), lanes)
    block = f32(half, rows, lanes)
    tiles = [
        pltpu.VMEM((levels, high + 2 * STEPS, lanes), jnp.float32),
        pltpu.VMEM((levels, high + 2 * STEPS, lanes), jnp.float32),
        pltpu.VMEM((levels, high + STEPS, lanes), jnp.float32),
        pltpu.VMEM((3 * half, rows + 2 * STEPS, lanes), jnp.float32),
    ]

    inputs = (
        vertical,
        alpha_fields,
        anomalies,
        lon_faces,
        lat_faces,
        normalizer,
        innovation,
        misfit_weight,
    )
    keep, give, alpha = pl.pallas_call(
        functools.partial(prepare_kernel, half),
        out_shape=(f32(6 * half, rows, lanes), f32(levels, rows, lanes), f32(*alpha_fields.shape)),
        in_specs=[HBM] * 8,
        out_specs=(VMEM, VMEM, VMEM),
        scratch_shapes=[
            pltpu.SMEM(vertical.shape, jnp.float32),
            pltpu.VMEM(anomalies.shape, jnp.float32),
            pltpu.VMEM(block.shape, jnp.float32),
            pltpu.VMEM(normalizer.shape, jnp.float32),
            pltpu.VMEM(block.shape, jnp.float32),
            pltpu.VMEM(misfit_weight.shape, jnp.float32),
            pltpu.SemaphoreType.DMA((8,)),
        ],
        compiler_params=PARAMS,
        name="prepare",
    )(*(pltpu.with_memory_space_constraint(value, pltpu.HBM) for value in inputs))
    got = around(give, "mem", 1)

    first, final = pl.pallas_call(
        functools.partial(strip_kernel, half),
        out_shape=(strip, strip),
        in_specs=[VMEM] * 2,
        out_specs=(VMEM,) * 2,
        compiler_params=PARAMS,
        name="strips",
    )(keep, got)
    below = around(final, "lon", 1)
    above = around(first, "lon", -1)
    west, east = pl.pallas_call(
        functools.partial(column_kernel, half),
        out_shape=(column, column),
        in_specs=[VMEM] * 4,
        out_specs=(VMEM,) * 2,
        compiler_params=PARAMS,
        name="columns",
    )(keep, got, below, above)
    left = around(east, "lat", 1)
    right = around(west, "lat", -1)
    edge_own = f32(high * 4 * half + (rows + 2 * STEPS) * 3 * half, lanes)
    main = pl.pallas_call(
        functools.partial(main_kernel, half),
        out_shape=(block, block, block, edge_own),
        in_specs=[VMEM] * 4,
        out_specs=(VMEM,) * 4,
        scratch_shapes=tiles,
        compiler_params=PARAMS,
        name="main",
    )(keep, got, below, above)
    increment, mine, theirs = pl.pallas_call(
        functools.partial(edge_kernel, half),
        out_shape=(block, block, block),
        in_specs=[VMEM] * 7,
        out_specs=(VMEM,) * 3,
        scratch_shapes=tiles + [pltpu.VMEM(block.shape, jnp.float32)],
        compiler_params=PARAMS,
        name="edge",
    )(keep, left, right, *main)
    got = around(theirs, "mem", 1)

    partial, splat = pl.pallas_call(
        functools.partial(partial_kernel, half),
        out_shape=(f32(levels, rows, lanes), f32(half, levels, lanes)),
        in_specs=[SMEM] + [VMEM] * 2,
        out_specs=(VMEM, VMEM),
        compiler_params=PARAMS,
        name="partial",
    )(vertical, alpha, mine)
    gradient = pl.pallas_call(
        functools.partial(gradient_kernel, half),
        out_shape=f32(*alpha_fields.shape),
        in_specs=[VMEM] * 3,
        out_specs=VMEM,
        compiler_params=PARAMS,
        name="gradient",
    )(partial, splat, got)
    return (increment, gradient)


def solution(mesh):
    return jax.shard_map(
        local,
        mesh=mesh,
        in_specs=(
            P("mem", None, "lon", "lat"),
            P("mem", None, "lon", "lat"),
            P(None, "lon", "lat"),
            P(None, "lon", "lat"),
            P(None, "lon", "lat"),
            P(None, "lon", "lat"),
            P(None, "lon", "lat"),
            P(),
        ),
        out_specs=(P("mem", "lon", "lat"), P("mem", None, "lon", "lat")),
        check_vma=False,
    )
```

```python
import functools
import math

import jax
import jax.numpy as jnp
from jax import lax
from jax.experimental import pallas as pl
from jax.experimental.pallas import tpu as pltpu
from jax.sharding import PartitionSpec as P

STEPS = 8
DEEP = 2 * STEPS
LANES = 128
TILE = 8
VMEM = pl.BlockSpec(memory_space=pltpu.VMEM)
SMEM = pl.BlockSpec(memory_space=pltpu.SMEM)
HBM = pl.BlockSpec(memory_space=pltpu.HBM)
PARAMS = pltpu.CompilerParams(vmem_limit_bytes=32 * 1024 * 1024)


def f32(*shape):
    return jax.ShapeDtypeStruct(shape, jnp.float32)


def around(value, axis, steps):
    count = lax.axis_size(axis)
    pairs = [(source, (source + steps) % count) for source in range(count)]
    return lax.ppermute(value, axis, pairs)


def lane_places(half):
    places = []
    for width, count in ((DEEP, 4 * half), (STEPS, 3 * half)):
        for i in range(count):
            group, place = divmod(i * width, LANES)
            if width == STEPS:
                group += -(-4 * half * DEEP // LANES)
            places.append((width, group, place, (place + 2 * DEEP - width) % LANES))
    return places


def turned(value, shift):
    shift = shift % value.shape[-1]
    return pltpu.roll(value, shift, axis=value.ndim - 1) if shift else value


def mixed(vertical_ref, alpha_ref, level):
    total = vertical_ref[level, 0] * alpha_ref[0, 0]
    for k in range(1, alpha_ref.shape[1]):
        total = total + vertical_ref[level, k] * alpha_ref[0, k]
    return total


def prepare_kernel(
    half,
    vertical_hbm,
    alpha_hbm,
    anomaly_hbm,
    lon_hbm,
    lat_hbm,
    normalizer_hbm,
    innovation_hbm,
    weight_hbm,
    keep,
    give,
    alpha,
    vertical,
    anomaly,
    faces,
    normalizer,
    innovation,
    weight,
    sems,
):
    base = lax.axis_index("mem") * half
    other = half - base
    pairs = [
        (vertical_hbm, vertical),
        (alpha_hbm, alpha),
        (weight_hbm, weight),
        (normalizer_hbm, normalizer),
        (anomaly_hbm, anomaly),
        (innovation_hbm.at[pl.ds(base, half)], innovation),
        (lon_hbm.at[pl.ds(base, half)], keep.at[pl.ds(half, half)]),
        (lat_hbm.at[pl.ds(base, half)], faces),
    ]
    copies = [pltpu.make_async_copy(a, b, sems.at[n]) for n, (a, b) in enumerate(pairs)]
    for copy in copies:
        copy.start()
    copies[0].wait()
    copies[1].wait()
    for i in range(half):
        keep[i] = mixed(vertical, alpha, base + i)
        give[i] = mixed(vertical, alpha, other + i)
    for copy in copies[2:]:
        copy.wait()
    last = lax.axis_index("lat") == lax.axis_size("lat") - 1
    lane = lax.broadcasted_iota(jnp.int32, faces.shape[1:], 1)
    closed = jnp.logical_and(last, lane == faces.shape[2] - 1)
    for i in range(half):
        mine, theirs = base + i, other + i
        root = jnp.sqrt(weight[mine])
        keep[2 * half + i] = jnp.where(closed, 0.0, faces[i])
        keep[3 * half + i] = normalizer[mine] * anomaly[0, mine] * root
        keep[4 * half + i] = root * innovation[i]
        keep[5 * half + i] = 1.0 / root
        give[half + i] = normalizer[theirs] * anomaly[0, theirs] * jnp.sqrt(weight[theirs])


def field_refs(half, keep, got):
    deep = [keep.at[i] for i in range(3 * half)] + [got.at[i] for i in range(half)]
    shallow = [keep.at[3 * half + i] for i in range(2 * half)]
    return deep + shallow + [got.at[half + i] for i in range(half)]


def widths(half):
    return [DEEP] * (4 * half) + [STEPS] * (3 * half)


def halo_refs(half, kept, gotten):
    refs = []
    ends = {False: 0, True: 0}
    for n, width in enumerate(widths(half)):
        late = 3 * half <= n < 4 * half or n >= 6 * half
        pack = gotten if late else kept
        refs.append(pack.at[pl.ds(ends[late], width)])
        ends[late] += width
    return refs


def strip_kernel(counts, source, first, final):
    rows = source.shape[1]
    at = 0
    n = 0
    for count, width in counts:
        for _ in range(count):
            first[at : at + width] = source[n, :width]
            final[at : at + width] = source[n, rows - width :]
            at += width
            n += 1


def in_lanes(lane, place, width):
    if place + width > LANES:
        return jnp.logical_or(lane >= place, lane < place + width - LANES)
    return jnp.logical_and(lane >= place, lane < place + width)


def column_kernel(half, keep, got, kept_below, got_below, kept_above, got_above, west, east):
    lanes = keep.shape[2]
    lane = lax.broadcasted_iota(jnp.int32, (1, lanes), 1)
    packs = {}
    for below, ref, above, (width, group, place, opposite) in zip(
        halo_refs(half, kept_below, got_below),
        field_refs(half, keep, got),
        halo_refs(half, kept_above, got_above),
        lane_places(half),
    ):
        for n, piece in enumerate((below[...], ref[...], above[...])):
            heads, tails = packs.get((group, n), (0.0, 0.0))
            heads = jnp.where(in_lanes(lane, place, width), turned(piece, place), heads)
            tails = jnp.where(in_lanes(lane, opposite, width), turned(piece, place + 2 * DEEP), tails)
            packs[group, n] = heads, tails
    at = 0
    for heads, tails in packs.values():
        count = heads.shape[0]
        west[at : at + count] = heads
        east[at : at + count] = tails
        at += count


def split_tiles(half, tiles):
    return tiles[:half], tiles[half : 2 * half], tiles[2 * half], tiles[2 * half + 1]


def diffusion(half, tiles, totals):
    fields, others, face_tiles, shallow_tiles = split_tiles(half, tiles)
    high = fields[0].shape[1] - 2 * STEPS
    rows = high - 2 * DEEP
    edge = jnp.zeros((STEPS, fields[0].shape[2]), jnp.float32)
    for n in range(2 * half):
        face_tiles[n, :STEPS] = edge
    for ref in (*fields, *others):
        for m in range(2):
            ref[m, :STEPS] = edge
            ref[m, STEPS + high :] = edge

    zero = lax.axis_index("mem") // 2

    def step(sources, targets, begin, end):
        for i in range(half):
            for at in range(begin, end, TILE):
                here = pl.ds(at, TILE)
                up = pl.ds(at + 1 + zero, TILE)
                down = pl.ds(at - 1 + zero, TILE)
                lon_coef = face_tiles[i, here]
                lon_before = face_tiles[i, down]
                lat_coef = face_tiles[half + i, here]
                lat_before = turned(lat_coef, 1)
                for m in range(2):
                    field = sources[i][m, here]
                    flux_x = lon_coef * (sources[i][m, up] - field)
                    flux_x = flux_x - lon_before * (field - sources[i][m, down])
                    flux_y = lat_coef * (turned(field, -1) - field)
                    flux_y = flux_y - lat_before * (field - turned(field, 1))
                    targets[i][m, here] = field + (flux_x + flux_y)

    def root(margin):
        begin, end = STEPS + margin, STEPS + high - margin

        def steps(_, carry):
            for _ in range(STEPS // 4):
                step(fields, others, begin, end)
                step(others, fields, begin, end)
            return carry

        lax.fori_loop(0, 2, steps, 0)

    root(0)
    inner = pl.ds(2 * STEPS, rows + 2 * STEPS)
    for i in range(half):
        gains = [shallow_tiles[i], shallow_tiles[2 * half + i]]
        total = gains[0] * fields[i][0, inner] + gains[1] * fields[i][1, inner]
        totals[i] = total[STEPS : STEPS + rows]
        residual = total - shallow_tiles[half + i]
        for m in range(2):
            fields[i][m, inner] = gains[m] * residual
    root(STEPS)


def tile_targets(half, tiles):
    fields, _, face_tiles, shallow_tiles = split_tiles(half, tiles)
    body = pl.ds(STEPS, fields[0].shape[1] - 2 * STEPS)
    targets = [fields[i].at[0, body] for i in range(half)]
    targets += [face_tiles.at[n, body] for n in range(2 * half)]
    targets += [fields[i].at[1, body] for i in range(half)]
    return targets + [shallow_tiles.at[n] for n in range(3 * half)]


def main_kernel(
    half,
    keep,
    got,
    kept_below,
    got_below,
    kept_above,
    got_above,
    total,
    mine,
    theirs,
    edge_own,
    *tiles,
):
    rows, lanes = keep.shape[1:]
    lane = lax.broadcasted_iota(jnp.int32, (1, lanes), 1)
    edge_at = 0
    for below, ref, above, out in zip(
        halo_refs(half, kept_below, got_below),
        field_refs(half, keep, got),
        halo_refs(half, kept_above, got_above),
        tile_targets(half, tiles),
    ):
        offset = 0
        for piece in (below[...], ref[...], above[...]):
            count = piece.shape[0]
            out[offset : offset + count] = piece
            own = jnp.where(lane < lanes - 3 * DEEP, turned(piece, 2 * DEEP), piece)
            edge_own[edge_at : edge_at + count] = own
            offset += count
            edge_at += count
    diffusion(half, tiles, total)
    own = pl.ds(STEPS + DEEP, rows)
    for i in range(half):
        mine[i] = tiles[i][0, own]
        theirs[i] = tiles[i][1, own]


def edge_kernel(
    half,
    keep,
    left,
    right,
    main_total,
    main_mine,
    main_theirs,
    edge_own,
    increment,
    mine,
    theirs,
    totals,
    *tiles,
):
    rows, lanes = keep.shape[1:]
    lane = lax.broadcasted_iota(jnp.int32, (1, lanes), 1)
    high = rows + 2 * DEEP
    at = 0
    for out, (width, group, place, _) in zip(tile_targets(half, tiles), lane_places(half)):
        count = rows + 2 * width
        here = pl.ds(group * high, count)
        sides = jnp.where(in_lanes(lane, place, width), right[here], left[here])
        out[...] = jnp.where(lane < 2 * DEEP, turned(sides, -place), edge_own[at : at + count])
        at += count
    diffusion(half, tiles, totals)
    body = pl.ds(STEPS + DEEP, rows)

    def joined(main, sides):
        sides = jnp.where(lane < DEEP, turned(sides, -2 * DEEP), sides)
        return jnp.where(in_lanes(lane, DEEP, lanes - 2 * DEEP), main, sides)

    for i in range(half):
        increment[i] = joined(main_total[i], totals[i]) * keep[5 * half + i]
        mine[i] = joined(main_mine[i], tiles[i][0, body])
        theirs[i] = joined(main_theirs[i], tiles[i][1, body])


def partial_kernel(half, vertical, alpha, mine, partial, splat):
    base = lax.axis_index("mem") * half
    other = half - base
    for k in range(2 * half):
        total = alpha[0, k]
        for i in range(half):
            total = total + vertical[base + i, k] * mine[i]
            splat[i, k : k + 1] = jnp.full((1, splat.shape[2]), vertical[other + i, k])
        partial[k] = total


def gradient_kernel(half, partial, splat, got, gradient):
    for k in range(2 * half):
        total = partial[k]
        for i in range(half):
            total = total + splat[i, k : k + 1] * got[i]
        gradient[0, k] = total


def local(
    alpha_fields, anomalies, lon_faces, lat_faces, normalizer, innovation, misfit_weight, vertical
):
    levels, rows, lanes = lon_faces.shape
    half = levels // 2
    high = rows + 2 * DEEP
    deep_groups = -(-4 * half * DEEP // lanes)
    shallow_groups = -(-3 * half * STEPS // lanes)
    column = f32(deep_groups * high + shallow_groups * (rows + 2 * STEPS), lanes)
    block = f32(half, rows, lanes)
    tiles = [pltpu.VMEM((2, high + 2 * STEPS, lanes), jnp.float32) for _ in range(2 * half)]
    tiles.append(pltpu.VMEM((levels, high + STEPS, lanes), jnp.float32))
    tiles.append(pltpu.VMEM((3 * half, rows + 2 * STEPS, lanes), jnp.float32))

    def strips(source, counts, name):
        strip = f32(sum(count * width for count, width in counts), lanes)
        first, final = pl.pallas_call(
            functools.partial(strip_kernel, counts),
            out_shape=(strip, strip),
            in_specs=[VMEM],
            out_specs=(VMEM,) * 2,
            compiler_params=PARAMS,
            name=name,
        )(source)
        return around(final, "lon", 1), around(first, "lon", -1)

    inputs = (
        vertical,
        alpha_fields,
        anomalies,
        lon_faces,
        lat_faces,
        normalizer,
        innovation,
        misfit_weight,
    )
    keep, give, alpha = pl.pallas_call(
        functools.partial(prepare_kernel, half),
        out_shape=(f32(6 * half, rows, lanes), f32(levels, rows, lanes), f32(*alpha_fields.shape)),
        in_specs=[HBM] * 8,
        out_specs=(VMEM, VMEM, VMEM),
        scratch_shapes=[
            pltpu.SMEM(vertical.shape, jnp.float32),
            pltpu.VMEM(anomalies.shape, jnp.float32),
            pltpu.VMEM(block.shape, jnp.float32),
            pltpu.VMEM(normalizer.shape, jnp.float32),
            pltpu.VMEM(block.shape, jnp.float32),
            pltpu.VMEM(misfit_weight.shape, jnp.float32),
            pltpu.SemaphoreType.DMA((8,)),
        ],
        compiler_params=PARAMS,
        name="prepare",
    )(*(pltpu.with_memory_space_constraint(value, pltpu.HBM) for value in inputs))
    got = around(give, "mem", 1)
    kept_below, kept_above = strips(keep, ((3 * half, DEEP), (2 * half, STEPS)), "kept_strips")
    got_below, got_above = strips(got, ((half, DEEP), (half, STEPS)), "got_strips")
    blocks = (keep, got, kept_below, got_below, kept_above, got_above)
    west, east = pl.pallas_call(
        functools.partial(column_kernel, half),
        out_shape=(column, column),
        in_specs=[VMEM] * 6,
        out_specs=(VMEM,) * 2,
        compiler_params=PARAMS,
        name="columns",
    )(*blocks)
    left = around(east, "lat", 1)
    right = around(west, "lat", -1)
    edge_own = f32(high * 4 * half + (rows + 2 * STEPS) * 3 * half, lanes)
    main = pl.pallas_call(
        functools.partial(main_kernel, half),
        out_shape=(block, block, block, edge_own),
        in_specs=[VMEM] * 6,
        out_specs=(VMEM,) * 4,
        scratch_shapes=tiles,
        compiler_params=PARAMS,
        name="main",
    )(*blocks)
    increment, mine, theirs = pl.pallas_call(
        functools.partial(edge_kernel, half),
        out_shape=(block, block, block),
        in_specs=[VMEM] * 7,
        out_specs=(VMEM,) * 3,
        scratch_shapes=[pltpu.VMEM(block.shape, jnp.float32)] + tiles,
        compiler_params=PARAMS,
        name="edge",
    )(keep, left, right, *main)
    got = around(theirs, "mem", 1)

    partial, splat = pl.pallas_call(
        functools.partial(partial_kernel, half),
        out_shape=(f32(levels, rows, lanes), f32(half, levels, lanes)),
        in_specs=[SMEM] + [VMEM] * 2,
        out_specs=(VMEM, VMEM),
        compiler_params=PARAMS,
        name="partial",
    )(vertical, alpha, mine)
    gradient = pl.pallas_call(
        functools.partial(gradient_kernel, half),
        out_shape=f32(*alpha_fields.shape),
        in_specs=[VMEM] * 3,
        out_specs=VMEM,
        compiler_params=PARAMS,
        name="gradient",
    )(partial, splat, got)
    return (increment, gradient)


def solution(mesh):
    return jax.shard_map(
        local,
        mesh=mesh,
        in_specs=(
            P("mem", None, "lon", "lat"),
            P("mem", None, "lon", "lat"),
            P(None, "lon", "lat"),
            P(None, "lon", "lat"),
            P(None, "lon", "lat"),
            P(None, "lon", "lat"),
            P(None, "lon", "lat"),
            P(),
        ),
        out_specs=(P("mem", "lon", "lat"), P("mem", None, "lon", "lat")),
        check_vma=False,
    )
```

```python
import functools
import math

import jax
import jax.numpy as jnp
from jax import lax
from jax.experimental import pallas as pl
from jax.experimental.pallas import tpu as pltpu
from jax.sharding import PartitionSpec as P

STEPS = 8
DEEP = 2 * STEPS
LANES = 128
TILE = 8
VMEM = pl.BlockSpec(memory_space=pltpu.VMEM)
SMEM = pl.BlockSpec(memory_space=pltpu.SMEM)
HBM = pl.BlockSpec(memory_space=pltpu.HBM)
PARAMS = pltpu.CompilerParams(vmem_limit_bytes=32 * 1024 * 1024)


def f32(*shape):
    return jax.ShapeDtypeStruct(shape, jnp.float32)


def around(value, axis, steps):
    count = lax.axis_size(axis)
    pairs = [(source, (source + steps) % count) for source in range(count)]
    return lax.ppermute(value, axis, pairs)


def lane_places(half):
    per = LANES // DEEP
    late = -(-3 * half // per)
    slots = [(DEEP, i // per, i % per * DEEP) for i in range(3 * half)]
    slots += [(DEEP, late, i * DEEP) for i in range(half)]
    slots += [(STEPS, late + 1, i * STEPS) for i in range(2 * half)]
    slots += [(STEPS, late, half * DEEP + i * STEPS) for i in range(half)]
    return [(width, n, at, (at + 2 * DEEP - width) % LANES) for width, n, at in slots]


def is_late(half, n):
    return 3 * half <= n < 4 * half or n >= 6 * half


def turned(value, shift):
    shift = shift % value.shape[-1]
    return pltpu.roll(value, shift, axis=value.ndim - 1) if shift else value


def mixed(vertical_ref, alpha_ref, level):
    total = vertical_ref[level, 0] * alpha_ref[0, 0]
    for k in range(1, alpha_ref.shape[1]):
        total = total + vertical_ref[level, k] * alpha_ref[0, k]
    return total


def prepare_kernel(
    half,
    vertical_hbm,
    alpha_hbm,
    anomaly_hbm,
    lon_hbm,
    lat_hbm,
    normalizer_hbm,
    innovation_hbm,
    weight_hbm,
    keep,
    give,
    alpha,
    vertical,
    anomaly,
    faces,
    normalizer,
    innovation,
    weight,
    sems,
):
    base = lax.axis_index("mem") * half
    other = half - base
    pairs = [
        (vertical_hbm, vertical),
        (alpha_hbm, alpha),
        (weight_hbm, weight),
        (normalizer_hbm, normalizer),
        (anomaly_hbm, anomaly),
        (innovation_hbm.at[pl.ds(base, half)], innovation),
        (lon_hbm.at[pl.ds(base, half)], keep.at[pl.ds(half, half)]),
        (lat_hbm.at[pl.ds(base, half)], faces),
    ]
    copies = [pltpu.make_async_copy(a, b, sems.at[n]) for n, (a, b) in enumerate(pairs)]
    for copy in copies:
        copy.start()
    copies[0].wait()
    copies[1].wait()
    for i in range(half):
        keep[i] = mixed(vertical, alpha, base + i)
        give[i] = mixed(vertical, alpha, other + i)
    for copy in copies[2:]:
        copy.wait()
    last = lax.axis_index("lat") == lax.axis_size("lat") - 1
    lane = lax.broadcasted_iota(jnp.int32, faces.shape[1:], 1)
    closed = jnp.logical_and(last, lane == faces.shape[2] - 1)
    for i in range(half):
        mine, theirs = base + i, other + i
        root = jnp.sqrt(weight[mine])
        keep[2 * half + i] = jnp.where(closed, 0.0, faces[i])
        keep[3 * half + i] = normalizer[mine] * anomaly[0, mine] * root
        keep[4 * half + i] = root * innovation[i]
        keep[5 * half + i] = 1.0 / root
        give[half + i] = normalizer[theirs] * anomaly[0, theirs] * jnp.sqrt(weight[theirs])


def field_refs(half, keep, got):
    deep = [keep.at[i] for i in range(3 * half)] + [got.at[i] for i in range(half)]
    shallow = [keep.at[3 * half + i] for i in range(2 * half)]
    return deep + shallow + [got.at[half + i] for i in range(half)]


def widths(half):
    return [DEEP] * (4 * half) + [STEPS] * (3 * half)


def halo_refs(half, kept, gotten):
    refs = []
    ends = {False: 0, True: 0}
    for n, width in enumerate(widths(half)):
        late = is_late(half, n)
        pack = gotten if late else kept
        refs.append(None if pack is None else pack.at[pl.ds(ends[late], width)])
        ends[late] += width
    return refs


def strip_kernel(counts, source, first, final):
    rows = source.shape[1]
    at = 0
    n = 0
    for count, width in counts:
        for _ in range(count):
            first[at : at + width] = source[n, :width]
            final[at : at + width] = source[n, rows - width :]
            at += width
            n += 1


def in_lanes(lane, place, width):
    if place + width > LANES:
        return jnp.logical_or(lane >= place, lane < place + width - LANES)
    return jnp.logical_and(lane >= place, lane < place + width)


def packed(half, lane, fields):
    packs = {}
    for n, rows in fields.items():
        width, group, place, opposite = lane_places(half)[n]
        heads, tails = packs.get(group, (jnp.zeros_like(rows), jnp.zeros_like(rows)))
        top = DEEP - width if rows.shape[0] < heads.shape[0] else 0
        if top:
            margin = jnp.zeros((top, rows.shape[1]), rows.dtype)
            rows = jnp.concatenate([margin, rows] if fields.low else [rows, margin], axis=0)
        heads = jnp.where(in_lanes(lane, place, width), turned(rows, place), heads)
        tails = jnp.where(in_lanes(lane, opposite, width), turned(rows, place + 2 * DEEP), tails)
        packs[group] = heads, tails
    return packs


class Side(dict):
    def __init__(self, items, low):
        super().__init__(items)
        self.low = low


def own_column_kernel(half, keep, got, west, east):
    lane = lax.broadcasted_iota(jnp.int32, (1, keep.shape[2]), 1)
    fields = {n: ref[...] for n, ref in enumerate(field_refs(half, keep, got))}
    for group, (heads, tails) in packed(half, lane, fields).items():
        west[group], east[group] = heads, tails


def halo_columns(half, lane, kept, gotten, low):
    refs = halo_refs(half, kept, gotten)
    chosen = {n: ref[...] for n, ref in enumerate(refs) if ref is not None}
    return packed(half, lane, Side(chosen, low))


def early_column_kernel(half, below, above, west, east):
    lane = lax.broadcasted_iota(jnp.int32, (1, below.shape[1]), 1)
    for side, ref in enumerate((below, above)):
        for group, (heads, tails) in halo_columns(half, lane, ref, None, side == 0).items():
            count = heads.shape[0]
            west[group, side, :count], east[group, side, :count] = heads, tails


def column_kernel(half, own_west, own_east, early_west, early_east, below, above, west, east):
    rows, lanes = own_west.shape[1:]
    lane = lax.broadcasted_iota(jnp.int32, (1, lanes), 1)
    late = [halo_columns(half, lane, None, ref, n == 0) for n, ref in enumerate((below, above))]
    groups = own_west.shape[0]
    for n, (own, early, out) in enumerate(((own_west, early_west, west), (own_east, early_east, east))):
        at = 0
        for group in range(groups):
            width = STEPS if group == groups - 1 else DEEP
            for side in range(2):
                place = at + side * (width + rows)
                ends = late[side][group][n] if group in late[side] else early[group, side, :width]
                out[place : place + width] = ends
            out[at + width : at + width + rows] = own[group]
            at += rows + 2 * width


def split_tiles(half, tiles):
    return tiles[:half], tiles[half : 2 * half], tiles[2 * half], tiles[2 * half + 1]


def diffusion(half, tiles, totals):
    fields, others, face_tiles, shallow_tiles = split_tiles(half, tiles)
    high = fields[0].shape[1] - 2 * STEPS
    rows = high - 2 * DEEP
    edge = jnp.zeros((STEPS, fields[0].shape[2]), jnp.float32)
    for n in range(2 * half):
        face_tiles[n, :STEPS] = edge
    for ref in (*fields, *others):
        for m in range(2):
            ref[m, :STEPS] = edge
            ref[m, STEPS + high :] = edge

    for i in range(half):
        face_tiles[2 * half + i, STEPS:] = turned(face_tiles[half + i, STEPS:], 1)

    zero = lax.axis_index("mem") // 2

    def step(sources, targets, begin, end):
        for i in range(half):
            for at in range(begin, end, TILE):
                here = pl.ds(at, TILE)
                up = pl.ds(at + 1 + zero, TILE)
                down = pl.ds(at - 1 + zero, TILE)
                lon_coef = face_tiles[i, here]
                lon_before = face_tiles[i, down]
                lat_coef = face_tiles[half + i, here]
                lat_before = face_tiles[2 * half + i, here]
                for m in range(2):
                    field = sources[i][m, here]
                    flux_x = lon_coef * (sources[i][m, up] - field)
                    flux_x = flux_x - lon_before * (field - sources[i][m, down])
                    flux_y = lat_coef * (turned(field, -1) - field)
                    flux_y = flux_y - lat_before * (field - turned(field, 1))
                    targets[i][m, here] = field + (flux_x + flux_y)

    def root(margin):
        begin, end = STEPS + margin, STEPS + high - margin

        def steps(_, carry):
            for _ in range(STEPS // 4):
                step(fields, others, begin, end)
                step(others, fields, begin, end)
            return carry

        lax.fori_loop(0, 2, steps, 0)

    root(0)
    inner = pl.ds(2 * STEPS, rows + 2 * STEPS)
    for i in range(half):
        gains = [shallow_tiles[i], shallow_tiles[2 * half + i]]
        total = gains[0] * fields[i][0, inner] + gains[1] * fields[i][1, inner]
        totals[i] = total[STEPS : STEPS + rows]
        residual = total - shallow_tiles[half + i]
        for m in range(2):
            fields[i][m, inner] = gains[m] * residual
    root(STEPS)


def tile_targets(half, tiles):
    fields, _, face_tiles, shallow_tiles = split_tiles(half, tiles)
    body = pl.ds(STEPS, fields[0].shape[1] - 2 * STEPS)
    targets = [fields[i].at[0, body] for i in range(half)]
    targets += [face_tiles.at[n, body] for n in range(2 * half)]
    targets += [fields[i].at[1, body] for i in range(half)]
    return targets + [shallow_tiles.at[n] for n in range(3 * half)]


def main_kernel(
    half,
    keep,
    got,
    kept_below,
    got_below,
    kept_above,
    got_above,
    total,
    mine,
    theirs,
    edge_own,
    *tiles,
):
    rows, lanes = keep.shape[1:]
    lane = lax.broadcasted_iota(jnp.int32, (1, lanes), 1)
    edge_at = 0
    for below, ref, above, out in zip(
        halo_refs(half, kept_below, got_below),
        field_refs(half, keep, got),
        halo_refs(half, kept_above, got_above),
        tile_targets(half, tiles),
    ):
        offset = 0
        for piece in (below[...], ref[...], above[...]):
            count = piece.shape[0]
            out[offset : offset + count] = piece
            own = jnp.where(lane < lanes - 3 * DEEP, turned(piece, 2 * DEEP), piece)
            edge_own[edge_at : edge_at + count] = own
            offset += count
            edge_at += count
    diffusion(half, tiles, total)
    own = pl.ds(STEPS + DEEP, rows)
    for i in range(half):
        mine[i] = tiles[i][0, own]
        theirs[i] = tiles[i][1, own]


def edge_kernel(
    half,
    keep,
    left,
    right,
    main_total,
    main_mine,
    main_theirs,
    edge_own,
    increment,
    mine,
    theirs,
    totals,
    *tiles,
):
    rows, lanes = keep.shape[1:]
    lane = lax.broadcasted_iota(jnp.int32, (1, lanes), 1)
    high = rows + 2 * DEEP
    groups = 1 + max(group for _, group, _, _ in lane_places(half))
    at = 0
    for out, (width, group, place, _) in zip(tile_targets(half, tiles), lane_places(half)):
        count = rows + 2 * width
        inset = DEEP - width if group < groups - 1 else 0
        here = pl.ds(group * high + inset, count)
        sides = jnp.where(in_lanes(lane, place, width), right[here], left[here])
        out[...] = jnp.where(lane < 2 * DEEP, turned(sides, -place), edge_own[at : at + count])
        at += count
    diffusion(half, tiles, totals)
    body = pl.ds(STEPS + DEEP, rows)

    def joined(main, sides):
        sides = jnp.where(lane < DEEP, turned(sides, -2 * DEEP), sides)
        return jnp.where(in_lanes(lane, DEEP, lanes - 2 * DEEP), main, sides)

    for i in range(half):
        increment[i] = joined(main_total[i], totals[i]) * keep[5 * half + i]
        mine[i] = joined(main_mine[i], tiles[i][0, body])
        theirs[i] = joined(main_theirs[i], tiles[i][1, body])


def partial_kernel(half, vertical, alpha, mine, partial, splat):
    base = lax.axis_index("mem") * half
    other = half - base
    for k in range(2 * half):
        total = alpha[0, k]
        for i in range(half):
            total = total + vertical[base + i, k] * mine[i]
            splat[i, k : k + 1] = jnp.full((1, splat.shape[2]), vertical[other + i, k])
        partial[k] = total


def gradient_kernel(half, partial, splat, got, gradient):
    for k in range(2 * half):
        total = partial[k]
        for i in range(half):
            total = total + splat[i, k : k + 1] * got[i]
        gradient[0, k] = total


def local(
    alpha_fields, anomalies, lon_faces, lat_faces, normalizer, innovation, misfit_weight, vertical
):
    levels, rows, lanes = lon_faces.shape
    half = levels // 2
    high = rows + 2 * DEEP
    groups = 1 + max(group for _, group, _, _ in lane_places(half))
    column = f32((groups - 1) * high + rows + 2 * STEPS, lanes)
    block = f32(half, rows, lanes)
    tiles = [pltpu.VMEM((2, high + 2 * STEPS, lanes), jnp.float32) for _ in range(2 * half)]
    tiles.append(pltpu.VMEM((3 * half, high + STEPS, lanes), jnp.float32))
    tiles.append(pltpu.VMEM((3 * half, rows + 2 * STEPS, lanes), jnp.float32))

    def strips(source, counts, name):
        strip = f32(sum(count * width for count, width in counts), lanes)
        first, final = pl.pallas_call(
            functools.partial(strip_kernel, counts),
            out_shape=(strip, strip),
            in_specs=[VMEM],
            out_specs=(VMEM,) * 2,
            compiler_params=PARAMS,
            name=name,
        )(source)
        return around(final, "lon", 1), around(first, "lon", -1)

    inputs = (
        vertical,
        alpha_fields,
        anomalies,
        lon_faces,
        lat_faces,
        normalizer,
        innovation,
        misfit_weight,
    )
    keep, give, alpha = pl.pallas_call(
        functools.partial(prepare_kernel, half),
        out_shape=(f32(6 * half, rows, lanes), f32(levels, rows, lanes), f32(*alpha_fields.shape)),
        in_specs=[HBM] * 8,
        out_specs=(VMEM, VMEM, VMEM),
        scratch_shapes=[
            pltpu.SMEM(vertical.shape, jnp.float32),
            pltpu.VMEM(anomalies.shape, jnp.float32),
            pltpu.VMEM(block.shape, jnp.float32),
            pltpu.VMEM(normalizer.shape, jnp.float32),
            pltpu.VMEM(block.shape, jnp.float32),
            pltpu.VMEM(misfit_weight.shape, jnp.float32),
            pltpu.SemaphoreType.DMA((8,)),
        ],
        compiler_params=PARAMS,
        name="prepare",
    )(*(pltpu.with_memory_space_constraint(value, pltpu.HBM) for value in inputs))
    got = around(give, "mem", 1)
    kept_below, kept_above = strips(keep, ((3 * half, DEEP), (2 * half, STEPS)), "kept_strips")
    got_below, got_above = strips(got, ((half, DEEP), (half, STEPS)), "got_strips")
    blocks = (keep, got, kept_below, got_below, kept_above, got_above)
    own_columns = pl.pallas_call(
        functools.partial(own_column_kernel, half),
        out_shape=(f32(groups, rows, lanes),) * 2,
        in_specs=[VMEM] * 2,
        out_specs=(VMEM,) * 2,
        compiler_params=PARAMS,
        name="own_columns",
    )(keep, got)
    early_columns = pl.pallas_call(
        functools.partial(early_column_kernel, half),
        out_shape=(f32(groups, 2, DEEP, lanes),) * 2,
        in_specs=[VMEM] * 2,
        out_specs=(VMEM,) * 2,
        compiler_params=PARAMS,
        name="early_columns",
    )(kept_below, kept_above)
    west, east = pl.pallas_call(
        functools.partial(column_kernel, half),
        out_shape=(column, column),
        in_specs=[VMEM] * 6,
        out_specs=(VMEM,) * 2,
        compiler_params=PARAMS,
        name="columns",
    )(*own_columns, *early_columns, got_below, got_above)
    left = around(east, "lat", 1)
    right = around(west, "lat", -1)
    edge_own = f32(high * 4 * half + (rows + 2 * STEPS) * 3 * half, lanes)
    main = pl.pallas_call(
        functools.partial(main_kernel, half),
        out_shape=(block, block, block, edge_own),
        in_specs=[VMEM] * 6,
        out_specs=(VMEM,) * 4,
        scratch_shapes=tiles,
        compiler_params=PARAMS,
        name="main",
    )(*blocks)
    increment, mine, theirs = pl.pallas_call(
        functools.partial(edge_kernel, half),
        out_shape=(block, block, block),
        in_specs=[VMEM] * 7,
        out_specs=(VMEM,) * 3,
        scratch_shapes=[pltpu.VMEM(block.shape, jnp.float32)] + tiles,
        compiler_params=PARAMS,
        name="edge",
    )(keep, left, right, *main)
    got = around(theirs, "mem", 1)

    partial, splat = pl.pallas_call(
        functools.partial(partial_kernel, half),
        out_shape=(f32(levels, rows, lanes), f32(half, levels, lanes)),
        in_specs=[SMEM] + [VMEM] * 2,
        out_specs=(VMEM, VMEM),
        compiler_params=PARAMS,
        name="partial",
    )(vertical, alpha, mine)
    gradient = pl.pallas_call(
        functools.partial(gradient_kernel, half),
        out_shape=f32(*alpha_fields.shape),
        in_specs=[VMEM] * 3,
        out_specs=VMEM,
        compiler_params=PARAMS,
        name="gradient",
    )(partial, splat, got)
    return (increment, gradient)


def solution(mesh):
    return jax.shard_map(
        local,
        mesh=mesh,
        in_specs=(
            P("mem", None, "lon", "lat"),
            P("mem", None, "lon", "lat"),
            P(None, "lon", "lat"),
            P(None, "lon", "lat"),
            P(None, "lon", "lat"),
            P(None, "lon", "lat"),
            P(None, "lon", "lat"),
            P(),
        ),
        out_specs=(P("mem", "lon", "lat"), P("mem", None, "lon", "lat")),
        check_vma=False,
    )
```

```python
import functools
import math

import jax
import jax.numpy as jnp
from jax import lax
from jax.experimental import pallas as pl
from jax.experimental.pallas import tpu as pltpu
from jax.sharding import PartitionSpec as P

STEPS = 8
DEEP = 2 * STEPS
LANES = 128
TILE = 8
VMEM = pl.BlockSpec(memory_space=pltpu.VMEM)
SMEM = pl.BlockSpec(memory_space=pltpu.SMEM)
HBM = pl.BlockSpec(memory_space=pltpu.HBM)
PARAMS = pltpu.CompilerParams(vmem_limit_bytes=32 * 1024 * 1024)


def f32(*shape):
    return jax.ShapeDtypeStruct(shape, jnp.float32)


def around(value, axis, steps):
    count = lax.axis_size(axis)
    pairs = [(source, (source + steps) % count) for source in range(count)]
    return lax.ppermute(value, axis, pairs)


def lane_places(half):
    halfway = LANES // 2
    places = [None] * (7 * half)
    pairs = [(i, 3 * half + i) for i in range(half)] + [(half + i, 2 * half + i) for i in range(half)]
    for k, pair in enumerate(pairs):
        group, at = divmod(k * DEEP, halfway)
        for side, n in enumerate(pair):
            places[n] = (DEEP, group, at + side * halfway)
    last = -(-len(pairs) * DEEP // halfway)
    for i in range(half):
        places[4 * half + i] = (STEPS, last, i * STEPS)
        places[6 * half + i] = (STEPS, last, i * STEPS + halfway)
        places[5 * half + i] = (STEPS, last, (half + i // 2) * STEPS + i % 2 * halfway)
    return places


def is_late(half, n):
    return 3 * half <= n < 4 * half or n >= 6 * half


def turned(value, shift):
    shift = shift % value.shape[-1]
    return pltpu.roll(value, shift, axis=value.ndim - 1) if shift else value


def mixed(vertical_ref, alpha_ref, level):
    total = vertical_ref[level, 0] * alpha_ref[0, 0]
    for k in range(1, alpha_ref.shape[1]):
        total = total + vertical_ref[level, k] * alpha_ref[0, k]
    return total


def prepare_kernel(
    half,
    vertical_hbm,
    alpha_hbm,
    anomaly_hbm,
    lon_hbm,
    lat_hbm,
    normalizer_hbm,
    innovation_hbm,
    weight_hbm,
    keep,
    give,
    alpha,
    vertical,
    anomaly,
    faces,
    normalizer,
    innovation,
    weight,
    sems,
):
    base = lax.axis_index("mem") * half
    other = half - base
    pairs = [
        (vertical_hbm, vertical),
        (alpha_hbm, alpha),
        (weight_hbm, weight),
        (normalizer_hbm, normalizer),
        (anomaly_hbm, anomaly),
        (innovation_hbm.at[pl.ds(base, half)], innovation),
        (lon_hbm.at[pl.ds(base, half)], keep.at[pl.ds(half, half)]),
        (lat_hbm.at[pl.ds(base, half)], faces),
    ]
    copies = [pltpu.make_async_copy(a, b, sems.at[n]) for n, (a, b) in enumerate(pairs)]
    for copy in copies:
        copy.start()
    copies[0].wait()
    copies[1].wait()
    for i in range(half):
        keep[i] = mixed(vertical, alpha, base + i)
        give[i] = mixed(vertical, alpha, other + i)
    for copy in copies[2:]:
        copy.wait()
    last = lax.axis_index("lat") == lax.axis_size("lat") - 1
    lane = lax.broadcasted_iota(jnp.int32, faces.shape[1:], 1)
    closed = jnp.logical_and(last, lane == faces.shape[2] - 1)
    for i in range(half):
        mine, theirs = base + i, other + i
        root = jnp.sqrt(weight[mine])
        keep[2 * half + i] = jnp.where(closed, 0.0, faces[i])
        keep[3 * half + i] = normalizer[mine] * anomaly[0, mine] * root
        keep[4 * half + i] = root * innovation[i]
        keep[5 * half + i] = 1.0 / root
        give[half + i] = normalizer[theirs] * anomaly[0, theirs] * jnp.sqrt(weight[theirs])


def field_refs(half, keep, got):
    deep = [keep.at[i] for i in range(3 * half)] + [got.at[i] for i in range(half)]
    shallow = [keep.at[3 * half + i] for i in range(2 * half)]
    return deep + shallow + [got.at[half + i] for i in range(half)]


def widths(half):
    return [DEEP] * (4 * half) + [STEPS] * (3 * half)


def halo_refs(half, kept, gotten):
    refs = []
    ends = {False: 0, True: 0}
    for n, width in enumerate(widths(half)):
        late = is_late(half, n)
        pack = gotten if late else kept
        refs.append(None if pack is None else pack.at[pl.ds(ends[late], width)])
        ends[late] += width
    return refs


def strip_kernel(counts, source, first, final):
    rows = source.shape[1]
    at = 0
    n = 0
    for count, width in counts:
        for _ in range(count):
            first[at : at + width] = source[n, :width]
            final[at : at + width] = source[n, rows - width :]
            at += width
            n += 1


def in_lanes(lane, place, width):
    return jnp.logical_and(lane >= place, lane < place + width)


def packed(half, lane, fields, packs):
    for n, rows in fields.items():
        width, group, place = lane_places(half)[n]
        heads, tails = packs.get(group, (jnp.zeros_like(rows), jnp.zeros_like(rows)))
        inside = in_lanes(lane, place, width)
        heads = jnp.where(inside, turned(rows, place), heads)
        tails = jnp.where(inside, turned(rows, place + width), tails)
        packs[group] = heads, tails
    return packs


def own_column_kernel(half, keep, got, west, east):
    lane = lax.broadcasted_iota(jnp.int32, (1, keep.shape[2]), 1)
    fields = {n: ref[...] for n, ref in enumerate(field_refs(half, keep, got))}
    for group, (heads, tails) in packed(half, lane, fields, {}).items():
        west[group], east[group] = heads, tails


def halo_columns(half, lane, kept, gotten, packs):
    refs = halo_refs(half, kept, gotten)
    fields = {n: ref[...] for n, ref in enumerate(refs) if ref is not None}
    return packed(half, lane, fields, packs)


def early_column_kernel(half, below, above, west, east):
    lane = lax.broadcasted_iota(jnp.int32, (1, below.shape[1]), 1)
    for side, ref in enumerate((below, above)):
        for group, (heads, tails) in halo_columns(half, lane, ref, None, {}).items():
            count = heads.shape[0]
            west[group, side, :count], east[group, side, :count] = heads, tails


def column_kernel(half, own_west, own_east, early_west, early_east, below, above, west, east):
    groups, rows, lanes = own_west.shape
    lane = lax.broadcasted_iota(jnp.int32, (1, lanes), 1)
    ends = []
    for side, ref in enumerate((below, above)):
        packs = {}
        for group in range(groups):
            here = pl.ds(0, STEPS if group == groups - 1 else DEEP)
            packs[group] = early_west[group, side, here], early_east[group, side, here]
        ends.append(halo_columns(half, lane, None, ref, packs))
    for n, (own, out) in enumerate(((own_west, west), (own_east, east))):
        at = 0
        for group in range(groups):
            for piece in (ends[0][group][n], own[group], ends[1][group][n]):
                count = piece.shape[0]
                out[at : at + count] = piece
                at += count


def split_tiles(half, tiles):
    return tiles[:half], tiles[half : 2 * half], tiles[2 * half], tiles[2 * half + 1]


def diffusion(half, tiles, totals):
    fields, others, face_tiles, shallow_tiles = split_tiles(half, tiles)
    copies = fields[0].shape[0]
    high = fields[0].shape[1] - 2 * STEPS
    rows = high - 2 * DEEP
    edge = jnp.zeros((STEPS, fields[0].shape[2]), jnp.float32)
    for n in range(2 * half):
        face_tiles[n, :STEPS] = edge
    for ref in (*fields, *others):
        for m in range(copies):
            ref[m, :STEPS] = edge
            ref[m, STEPS + high :] = edge

    for i in range(half):
        face_tiles[2 * half + i, STEPS:] = turned(face_tiles[half + i, STEPS:], 1)

    zero = lax.axis_index("mem") // 2

    def step(sources, targets, begin, end):
        for i in range(half):
            for at in range(begin, end, TILE):
                here = pl.ds(at, TILE)
                up = pl.ds(at + 1 + zero, TILE)
                down = pl.ds(at - 1 + zero, TILE)
                lon_coef = face_tiles[i, here]
                lon_before = face_tiles[i, down]
                lat_coef = face_tiles[half + i, here]
                lat_before = face_tiles[2 * half + i, here]
                for m in range(copies):
                    field = sources[i][m, here]
                    flux_x = lon_coef * (sources[i][m, up] - field)
                    flux_x = flux_x - lon_before * (field - sources[i][m, down])
                    flux_y = lat_coef * (turned(field, -1) - field)
                    flux_y = flux_y - lat_before * (field - turned(field, 1))
                    targets[i][m, here] = field + (flux_x + flux_y)

    def root(margin):
        begin, end = STEPS + margin, STEPS + high - margin

        def steps(_, carry):
            for _ in range(STEPS // 4):
                step(fields, others, begin, end)
                step(others, fields, begin, end)
            return carry

        lax.fori_loop(0, 2, steps, 0)

    root(0)
    inner = pl.ds(2 * STEPS, rows + 2 * STEPS)
    for i in range(half):
        gains = [shallow_tiles[2 * m * half + i] for m in range(copies)]
        parts = [gains[m] * fields[i][m, inner] for m in range(copies)]
        total = parts[0] + (parts[1] if copies == 2 else turned(parts[0], LANES // 2))
        totals[i] = total[STEPS : STEPS + rows]
        residual = total - shallow_tiles[half + i]
        for m in range(copies):
            fields[i][m, inner] = gains[m] * residual
    root(STEPS)


def tile_targets(half, tiles):
    fields, _, face_tiles, shallow_tiles = split_tiles(half, tiles)
    body = pl.ds(STEPS, fields[0].shape[1] - 2 * STEPS)
    targets = [fields[i].at[0, body] for i in range(half)]
    targets += [face_tiles.at[n, body] for n in range(2 * half)]
    if fields[0].shape[0] == 2:
        targets += [fields[i].at[1, body] for i in range(half)]
    return targets + [shallow_tiles.at[n] for n in range(shallow_tiles.shape[0])]


def main_kernel(
    half,
    keep,
    got,
    kept_below,
    got_below,
    kept_above,
    got_above,
    total,
    mine,
    theirs,
    left_own,
    right_own,
    *tiles,
):
    rows, lanes = keep.shape[1:]
    lane = lax.broadcasted_iota(jnp.int32, (1, lanes), 1)
    targets = tile_targets(half, tiles)
    for below, ref, above, out in zip(
        halo_refs(half, kept_below, got_below),
        field_refs(half, keep, got),
        halo_refs(half, kept_above, got_above),
        targets,
    ):
        offset = 0
        for piece in (below[...], ref[...], above[...]):
            count = piece.shape[0]
            out[offset : offset + count] = piece
            offset += count
    pairs = [(n, 3 * half + n if n < half else n) for n in range(3 * half)]
    pairs += [(4 * half + i, 6 * half + i) for i in range(half)]
    pairs += [(5 * half + i, 5 * half + i) for i in range(half)]
    halfway = lanes // 2
    at = 0
    for one, two in pairs:
        a, b = targets[one][...], targets[two][...]
        count = a.shape[0]
        here = pl.ds(at, count)
        left_own[here] = jnp.where(lane < halfway, turned(a, DEEP), turned(b, DEEP + halfway))
        right_own[here] = jnp.where(lane < halfway, turned(a, halfway - DEEP), turned(b, -DEEP))
        at += count
    diffusion(half, tiles, total)
    own = pl.ds(STEPS + DEEP, rows)
    for i in range(half):
        mine[i] = tiles[i][0, own]
        theirs[i] = tiles[i][1, own]


def edge_kernel(
    half, after, pack, own, total_in, mine_in, theirs_in, total_out, mine, theirs, totals, *tiles
):
    rows, lanes = mine.shape[1:]
    high = rows + 2 * DEEP
    halfway = lanes // 2
    lane = lax.broadcasted_iota(jnp.int32, (1, lanes), 1)
    begin = halfway - DEEP if after else 0
    inside = jnp.logical_or(
        in_lanes(lane, begin, DEEP), in_lanes(lane, begin + halfway, DEEP)
    )
    low = lane < halfway
    places = lane_places(half)
    targets = tile_targets(half, tiles)

    def sides(n):
        width, group, place = places[n]
        shift = begin + (0 if after else DEEP - width) - place % halfway
        return turned(pack[pl.ds(group * high, rows + 2 * width)], shift)

    blocks = [sides(i) for i in range(half)]
    faces = [sides(half + i) for i in range(half)]
    swapped = [turned(block, halfway) for block in faces]
    blocks += [jnp.where(low, a, b) for a, b in zip(faces, swapped)]
    blocks += [jnp.where(low, b, a) for a, b in zip(faces, swapped)]
    blocks += [sides(4 * half + i) for i in range(half)]
    for i in range(half):
        a = sides(5 * half + i)
        b = turned(a, halfway)
        blocks.append(jnp.where(low, b, a) if i % 2 else jnp.where(low, a, b))
    at = 0
    for block, out in zip(blocks, targets):
        count = block.shape[0]
        out[...] = jnp.where(inside, block, own[at : at + count])
        at += count
    diffusion(half, tiles, totals)
    body = pl.ds(STEPS + DEEP, rows)
    shift = halfway + DEEP if after else -DEEP
    chosen = lane >= lanes - DEEP if after else lane < DEEP
    for i in range(half):
        field = tiles[i][0, body]
        total_out[i] = jnp.where(chosen, turned(totals[i], shift), total_in[i])
        mine[i] = jnp.where(chosen, turned(field, shift), mine_in[i])
        theirs[i] = jnp.where(chosen, turned(field, shift + halfway), theirs_in[i])


def last_edge_kernel(half, keep, pack, own, total_in, mine_in, theirs_in, increment, *rest):
    edge_kernel(half, True, pack, own, total_in, mine_in, theirs_in, increment, *rest)
    for i in range(half):
        increment[i] = increment[i] * keep[5 * half + i]


def partial_kernel(half, vertical, alpha, mine, partial, splat):
    base = lax.axis_index("mem") * half
    other = half - base
    for k in range(2 * half):
        total = alpha[0, k]
        for i in range(half):
            total = total + vertical[base + i, k] * mine[i]
            splat[i, k : k + 1] = jnp.full((1, splat.shape[2]), vertical[other + i, k])
        partial[k] = total


def gradient_kernel(half, partial, splat, got, gradient):
    for k in range(2 * half):
        total = partial[k]
        for i in range(half):
            total = total + splat[i, k : k + 1] * got[i]
        gradient[0, k] = total


def local(
    alpha_fields, anomalies, lon_faces, lat_faces, normalizer, innovation, misfit_weight, vertical
):
    levels, rows, lanes = lon_faces.shape
    half = levels // 2
    high = rows + 2 * DEEP
    groups = 1 + max(group for _, group, _ in lane_places(half))
    column = f32((groups - 1) * high + rows + 2 * STEPS, lanes)
    block = f32(half, rows, lanes)

    def tiles(copies):
        shapes = [(copies, high + 2 * STEPS, lanes)] * (2 * half)
        shapes.append((3 * half, high + STEPS, lanes))
        shapes.append(((1 + copies) * half, rows + 2 * STEPS, lanes))
        return [pltpu.VMEM(shape, jnp.float32) for shape in shapes]

    def strips(source, counts, name):
        strip = f32(sum(count * width for count, width in counts), lanes)
        first, final = pl.pallas_call(
            functools.partial(strip_kernel, counts),
            out_shape=(strip, strip),
            in_specs=[VMEM],
            out_specs=(VMEM,) * 2,
            compiler_params=PARAMS,
            name=name,
        )(source)
        return around(final, "lon", 1), around(first, "lon", -1)

    inputs = (
        vertical,
        alpha_fields,
        anomalies,
        lon_faces,
        lat_faces,
        normalizer,
        innovation,
        misfit_weight,
    )
    keep, give, alpha = pl.pallas_call(
        functools.partial(prepare_kernel, half),
        out_shape=(f32(6 * half, rows, lanes), f32(levels, rows, lanes), f32(*alpha_fields.shape)),
        in_specs=[HBM] * 8,
        out_specs=(VMEM, VMEM, VMEM),
        scratch_shapes=[
            pltpu.SMEM(vertical.shape, jnp.float32),
            pltpu.VMEM(anomalies.shape, jnp.float32),
            pltpu.VMEM(block.shape, jnp.float32),
            pltpu.VMEM(normalizer.shape, jnp.float32),
            pltpu.VMEM(block.shape, jnp.float32),
            pltpu.VMEM(misfit_weight.shape, jnp.float32),
            pltpu.SemaphoreType.DMA((8,)),
        ],
        compiler_params=PARAMS,
        name="prepare",
    )(*(pltpu.with_memory_space_constraint(value, pltpu.HBM) for value in inputs))
    got = around(give, "mem", 1)
    kept_below, kept_above = strips(keep, ((3 * half, DEEP), (2 * half, STEPS)), "kept_strips")
    got_below, got_above = strips(got, ((half, DEEP), (half, STEPS)), "got_strips")
    blocks = (keep, got, kept_below, got_below, kept_above, got_above)
    own_columns = pl.pallas_call(
        functools.partial(own_column_kernel, half),
        out_shape=(f32(groups, rows, lanes),) * 2,
        in_specs=[VMEM] * 2,
        out_specs=(VMEM,) * 2,
        compiler_params=PARAMS,
        name="own_columns",
    )(keep, got)
    early_columns = pl.pallas_call(
        functools.partial(early_column_kernel, half),
        out_shape=(f32(groups, 2, DEEP, lanes),) * 2,
        in_specs=[VMEM] * 2,
        out_specs=(VMEM,) * 2,
        compiler_params=PARAMS,
        name="early_columns",
    )(kept_below, kept_above)
    west, east = pl.pallas_call(
        functools.partial(column_kernel, half),
        out_shape=(column, column),
        in_specs=[VMEM] * 6,
        out_specs=(VMEM,) * 2,
        compiler_params=PARAMS,
        name="columns",
    )(*own_columns, *early_columns, got_below, got_above)
    left = around(east, "lat", 1)
    right = around(west, "lat", -1)
    edge_own = f32(high * 3 * half + (rows + 2 * STEPS) * 2 * half, lanes)
    *main, left_own, right_own = pl.pallas_call(
        functools.partial(main_kernel, half),
        out_shape=(block, block, block, edge_own, edge_own),
        in_specs=[VMEM] * 6,
        out_specs=(VMEM,) * 5,
        scratch_shapes=tiles(2),
        compiler_params=PARAMS,
        name="main",
    )(*blocks)
    edge_tiles = [pltpu.VMEM(block.shape, jnp.float32)] + tiles(1)
    joined = pl.pallas_call(
        functools.partial(edge_kernel, half, False),
        out_shape=(block, block, block),
        in_specs=[VMEM] * 5,
        out_specs=(VMEM,) * 3,
        scratch_shapes=edge_tiles,
        compiler_params=PARAMS,
        name="left_edge",
    )(left, left_own, *main)
    increment, mine, theirs = pl.pallas_call(
        functools.partial(last_edge_kernel, half),
        out_shape=(block, block, block),
        in_specs=[VMEM] * 6,
        out_specs=(VMEM,) * 3,
        scratch_shapes=edge_tiles,
        compiler_params=PARAMS,
        name="right_edge",
    )(keep, right, right_own, *joined)
    got = around(theirs, "mem", 1)

    partial, splat = pl.pallas_call(
        functools.partial(partial_kernel, half),
        out_shape=(f32(levels, rows, lanes), f32(half, levels, lanes)),
        in_specs=[SMEM] + [VMEM] * 2,
        out_specs=(VMEM, VMEM),
        compiler_params=PARAMS,
        name="partial",
    )(vertical, alpha, mine)
    gradient = pl.pallas_call(
        functools.partial(gradient_kernel, half),
        out_shape=f32(*alpha_fields.shape),
        in_specs=[VMEM] * 3,
        out_specs=VMEM,
        compiler_params=PARAMS,
        name="gradient",
    )(partial, splat, got)
    return (increment, gradient)


def solution(mesh):
    return jax.shard_map(
        local,
        mesh=mesh,
        in_specs=(
            P("mem", None, "lon", "lat"),
            P("mem", None, "lon", "lat"),
            P(None, "lon", "lat"),
            P(None, "lon", "lat"),
            P(None, "lon", "lat"),
            P(None, "lon", "lat"),
            P(None, "lon", "lat"),
            P(),
        ),
        out_specs=(P("mem", "lon", "lat"), P("mem", None, "lon", "lat")),
        check_vma=False,
    )
```

```python
import functools
import math

import jax
import jax.numpy as jnp
from jax import lax
from jax.experimental import pallas as pl
from jax.experimental.pallas import tpu as pltpu
from jax.sharding import PartitionSpec as P

STEPS = 8
DEEP = 2 * STEPS
LANES = 128
TILE = 8
VMEM = pl.BlockSpec(memory_space=pltpu.VMEM)
SMEM = pl.BlockSpec(memory_space=pltpu.SMEM)
HBM = pl.BlockSpec(memory_space=pltpu.HBM)
PARAMS = pltpu.CompilerParams(vmem_limit_bytes=32 * 1024 * 1024)


def f32(*shape):
    return jax.ShapeDtypeStruct(shape, jnp.float32)


def around(value, axis, steps):
    count = lax.axis_size(axis)
    pairs = [(source, (source + steps) % count) for source in range(count)]
    return lax.ppermute(value, axis, pairs)


def lane_places(half):
    per = LANES // DEEP
    late = -(-3 * half // per)
    slots = [(DEEP, i // per, i % per * DEEP) for i in range(3 * half)]
    slots += [(DEEP, late, i * DEEP) for i in range(half)]
    slots += [(STEPS, late + 1, i * STEPS) for i in range(2 * half)]
    slots += [(STEPS, late, half * DEEP + i * STEPS) for i in range(half)]
    return [(width, n, at, (at + 2 * DEEP - width) % LANES) for width, n, at in slots]


def is_late(half, n):
    return 3 * half <= n < 4 * half or n >= 6 * half


def turned(value, shift):
    shift = shift % value.shape[-1]
    return pltpu.roll(value, shift, axis=value.ndim - 1) if shift else value


def mixed(vertical_ref, alpha_ref, level):
    total = vertical_ref[level, 0] * alpha_ref[0, 0]
    for k in range(1, alpha_ref.shape[1]):
        total = total + vertical_ref[level, k] * alpha_ref[0, k]
    return total


def prepare_kernel(
    half,
    vertical_hbm,
    alpha_hbm,
    anomaly_hbm,
    lon_hbm,
    lat_hbm,
    normalizer_hbm,
    innovation_hbm,
    weight_hbm,
    keep,
    give,
    alpha,
    vertical,
    anomaly,
    faces,
    normalizer,
    innovation,
    weight,
    sems,
):
    base = lax.axis_index("mem") * half
    other = half - base
    pairs = [
        (vertical_hbm, vertical),
        (alpha_hbm, alpha),
        (weight_hbm, weight),
        (normalizer_hbm, normalizer),
        (anomaly_hbm, anomaly),
        (innovation_hbm.at[pl.ds(base, half)], innovation),
        (lon_hbm.at[pl.ds(base, half)], keep.at[pl.ds(half, half)]),
        (lat_hbm.at[pl.ds(base, half)], faces),
    ]
    copies = [pltpu.make_async_copy(a, b, sems.at[n]) for n, (a, b) in enumerate(pairs)]
    for copy in copies:
        copy.start()
    copies[0].wait()
    copies[1].wait()
    for i in range(half):
        keep[i] = mixed(vertical, alpha, base + i)
        give[i] = mixed(vertical, alpha, other + i)
    for copy in copies[2:]:
        copy.wait()
    last = lax.axis_index("lat") == lax.axis_size("lat") - 1
    lane = lax.broadcasted_iota(jnp.int32, faces.shape[1:], 1)
    closed = jnp.logical_and(last, lane == faces.shape[2] - 1)
    for i in range(half):
        mine, theirs = base + i, other + i
        root = jnp.sqrt(weight[mine])
        keep[2 * half + i] = jnp.where(closed, 0.0, faces[i])
        keep[3 * half + i] = normalizer[mine] * anomaly[0, mine] * root
        keep[4 * half + i] = root * innovation[i]
        keep[5 * half + i] = 1.0 / root
        give[half + i] = normalizer[theirs] * anomaly[0, theirs] * jnp.sqrt(weight[theirs])


def field_refs(half, keep, got):
    deep = [keep.at[i] for i in range(3 * half)] + [got.at[i] for i in range(half)]
    shallow = [keep.at[3 * half + i] for i in range(2 * half)]
    return deep + shallow + [got.at[half + i] for i in range(half)]


def widths(half):
    return [DEEP] * (4 * half) + [STEPS] * (3 * half)


def halo_refs(half, kept, gotten):
    refs = []
    ends = {False: 0, True: 0}
    for n, width in enumerate(widths(half)):
        late = is_late(half, n)
        pack = gotten if late else kept
        refs.append(None if pack is None else pack.at[pl.ds(ends[late], width)])
        ends[late] += width
    return refs


def strip_kernel(counts, source, first, final):
    rows = source.shape[1]
    at = 0
    n = 0
    for count, width in counts:
        for _ in range(count):
            first[at : at + width] = source[n, :width]
            final[at : at + width] = source[n, rows - width :]
            at += width
            n += 1


def in_lanes(lane, place, width):
    if place + width > LANES:
        return jnp.logical_or(lane >= place, lane < place + width - LANES)
    return jnp.logical_and(lane >= place, lane < place + width)


def packed(half, lane, fields):
    packs = {}
    for n, rows in fields.items():
        width, group, place, opposite = lane_places(half)[n]
        heads, tails = packs.get(group, (jnp.zeros_like(rows), jnp.zeros_like(rows)))
        top = DEEP - width if rows.shape[0] < heads.shape[0] else 0
        if top:
            margin = jnp.zeros((top, rows.shape[1]), rows.dtype)
            rows = jnp.concatenate([margin, rows] if fields.low else [rows, margin], axis=0)
        heads = jnp.where(in_lanes(lane, place, width), turned(rows, place), heads)
        tails = jnp.where(in_lanes(lane, opposite, width), turned(rows, place + 2 * DEEP), tails)
        packs[group] = heads, tails
    return packs


class Side(dict):
    def __init__(self, items, low):
        super().__init__(items)
        self.low = low


def own_column_kernel(half, keep, got, west, east):
    lane = lax.broadcasted_iota(jnp.int32, (1, keep.shape[2]), 1)
    fields = {n: ref[...] for n, ref in enumerate(field_refs(half, keep, got))}
    for group, (heads, tails) in packed(half, lane, fields).items():
        west[group], east[group] = heads, tails


def halo_columns(half, lane, kept, gotten, low):
    refs = halo_refs(half, kept, gotten)
    chosen = {n: ref[...] for n, ref in enumerate(refs) if ref is not None}
    return packed(half, lane, Side(chosen, low))


def early_column_kernel(half, below, above, west, east):
    lane = lax.broadcasted_iota(jnp.int32, (1, below.shape[1]), 1)
    for side, ref in enumerate((below, above)):
        for group, (heads, tails) in halo_columns(half, lane, ref, None, side == 0).items():
            count = heads.shape[0]
            west[group, side, :count], east[group, side, :count] = heads, tails


def column_kernel(half, own_west, own_east, early_west, early_east, below, above, west, east):
    rows, lanes = own_west.shape[1:]
    lane = lax.broadcasted_iota(jnp.int32, (1, lanes), 1)
    late = [halo_columns(half, lane, None, ref, n == 0) for n, ref in enumerate((below, above))]
    groups = own_west.shape[0]
    for n, (own, early, out) in enumerate(((own_west, early_west, west), (own_east, early_east, east))):
        at = 0
        for group in range(groups):
            width = STEPS if group == groups - 1 else DEEP
            for side in range(2):
                place = at + side * (width + rows)
                ends = late[side][group][n] if group in late[side] else early[group, side, :width]
                out[place : place + width] = ends
            out[at + width : at + width + rows] = own[group]
            at += rows + 2 * width


def split_tiles(half, tiles):
    return tiles[:half], tiles[half : 2 * half], tiles[2 * half], tiles[2 * half + 1]


def diffusion(half, tiles, totals, straight):
    fields, others, face_tiles, shallow_tiles = split_tiles(half, tiles)
    high = fields[0].shape[1] - 2 * STEPS
    rows = high - 2 * DEEP
    edge = jnp.zeros((STEPS, fields[0].shape[2]), jnp.float32)
    for n in range(2 * half):
        face_tiles[n, :STEPS] = edge
    for ref in (*fields, *others):
        for m in range(2):
            ref[m, :STEPS] = edge
            ref[m, STEPS + high :] = edge

    for i in range(half):
        face_tiles[2 * half + i, STEPS:] = turned(face_tiles[half + i, STEPS:], 1)

    zero = lax.axis_index("mem") // 2

    def step(sources, targets, begin, end):
        for i in range(half):
            for at in range(begin, end, TILE):
                here = pl.ds(at, TILE)
                up = pl.ds(at + 1 + zero, TILE)
                down = pl.ds(at - 1 + zero, TILE)
                lon_coef = face_tiles[i, here]
                lon_before = face_tiles[i, down]
                lat_coef = face_tiles[half + i, here]
                lat_before = face_tiles[2 * half + i, here]
                for m in range(2):
                    field = sources[i][m, here]
                    flux_x = lon_coef * (sources[i][m, up] - field)
                    flux_x = flux_x - lon_before * (field - sources[i][m, down])
                    flux_y = lat_coef * (turned(field, -1) - field)
                    flux_y = flux_y - lat_before * (field - turned(field, 1))
                    targets[i][m, here] = field + (flux_x + flux_y)

    def root(margin):
        begin, end = STEPS + margin, STEPS + high - margin
        if straight:
            refs = fields, others
            for n in range(STEPS):
                cut = TILE if n == STEPS - 1 else 0
                step(refs[n % 2], refs[1 - n % 2], begin + cut, end - cut)
            return

        def steps(_, carry):
            for _ in range(STEPS // 4):
                step(fields, others, begin, end)
                step(others, fields, begin, end)
            return carry

        lax.fori_loop(0, 2, steps, 0)

    root(0)
    inner = pl.ds(2 * STEPS, rows + 2 * STEPS)
    for i in range(half):
        gains = [shallow_tiles[i], shallow_tiles[2 * half + i]]
        total = gains[0] * fields[i][0, inner] + gains[1] * fields[i][1, inner]
        totals[i] = total[STEPS : STEPS + rows]
        residual = total - shallow_tiles[half + i]
        for m in range(2):
            fields[i][m, inner] = gains[m] * residual
    root(STEPS)


def tile_targets(half, tiles):
    fields, _, face_tiles, shallow_tiles = split_tiles(half, tiles)
    body = pl.ds(STEPS, fields[0].shape[1] - 2 * STEPS)
    targets = [fields[i].at[0, body] for i in range(half)]
    targets += [face_tiles.at[n, body] for n in range(2 * half)]
    targets += [fields[i].at[1, body] for i in range(half)]
    return targets + [shallow_tiles.at[n] for n in range(3 * half)]


def main_kernel(
    half,
    keep,
    got,
    kept_below,
    got_below,
    kept_above,
    got_above,
    total,
    mine,
    theirs,
    edge_own,
    *tiles,
):
    rows, lanes = keep.shape[1:]
    lane = lax.broadcasted_iota(jnp.int32, (1, lanes), 1)
    edge_at = 0
    for below, ref, above, out in zip(
        halo_refs(half, kept_below, got_below),
        field_refs(half, keep, got),
        halo_refs(half, kept_above, got_above),
        tile_targets(half, tiles),
    ):
        offset = 0
        for piece in (below[...], ref[...], above[...]):
            count = piece.shape[0]
            out[offset : offset + count] = piece
            own = jnp.where(lane < lanes - 3 * DEEP, turned(piece, 2 * DEEP), piece)
            edge_own[edge_at : edge_at + count] = own
            offset += count
            edge_at += count
    diffusion(half, tiles, total, False)
    own = pl.ds(STEPS + DEEP, rows)
    for i in range(half):
        mine[i] = tiles[i][0, own]
        theirs[i] = tiles[i][1, own]


def edge_kernel(
    half,
    left,
    right,
    main_total,
    main_mine,
    main_theirs,
    edge_own,
    total,
    mine,
    theirs,
    totals,
    *tiles,
):
    rows, lanes = mine.shape[1:]
    lane = lax.broadcasted_iota(jnp.int32, (1, lanes), 1)
    high = rows + 2 * DEEP
    groups = 1 + max(group for _, group, _, _ in lane_places(half))
    at = 0
    for out, (width, group, place, _) in zip(tile_targets(half, tiles), lane_places(half)):
        count = rows + 2 * width
        inset = DEEP - width if group < groups - 1 else 0
        here = pl.ds(group * high + inset, count)
        sides = jnp.where(in_lanes(lane, place, width), right[here], left[here])
        out[...] = jnp.where(lane < 2 * DEEP, turned(sides, -place), edge_own[at : at + count])
        at += count
    diffusion(half, tiles, totals, True)
    body = pl.ds(STEPS + DEEP, rows)

    def joined(main, sides):
        sides = jnp.where(lane < DEEP, turned(sides, -2 * DEEP), sides)
        return jnp.where(in_lanes(lane, DEEP, lanes - 2 * DEEP), main, sides)

    for i in range(half):
        total[i] = joined(main_total[i], totals[i])
        mine[i] = joined(main_mine[i], tiles[i][0, body])
        theirs[i] = joined(main_theirs[i], tiles[i][1, body])


def partial_kernel(half, vertical, alpha, mine, keep, total, partial, splat, increment):
    for i in range(half):
        increment[i] = total[i] * keep[5 * half + i]
    base = lax.axis_index("mem") * half
    other = half - base
    for k in range(2 * half):
        result = alpha[0, k]
        for i in range(half):
            result = result + vertical[base + i, k] * mine[i]
            splat[i, k : k + 1] = jnp.full((1, splat.shape[2]), vertical[other + i, k])
        partial[k] = result


def gradient_kernel(half, partial, splat, got, gradient):
    for k in range(2 * half):
        total = partial[k]
        for i in range(half):
            total = total + splat[i, k : k + 1] * got[i]
        gradient[0, k] = total


def local(
    alpha_fields, anomalies, lon_faces, lat_faces, normalizer, innovation, misfit_weight, vertical
):
    levels, rows, lanes = lon_faces.shape
    half = levels // 2
    high = rows + 2 * DEEP
    groups = 1 + max(group for _, group, _, _ in lane_places(half))
    column = f32((groups - 1) * high + rows + 2 * STEPS, lanes)
    block = f32(half, rows, lanes)
    tiles = [pltpu.VMEM((2, high + 2 * STEPS, lanes), jnp.float32) for _ in range(2 * half)]
    tiles.append(pltpu.VMEM((3 * half, high + STEPS, lanes), jnp.float32))
    tiles.append(pltpu.VMEM((3 * half, rows + 2 * STEPS, lanes), jnp.float32))

    def strips(source, counts, name):
        strip = f32(sum(count * width for count, width in counts), lanes)
        first, final = pl.pallas_call(
            functools.partial(strip_kernel, counts),
            out_shape=(strip, strip),
            in_specs=[VMEM],
            out_specs=(VMEM,) * 2,
            compiler_params=PARAMS,
            name=name,
        )(source)
        return around(final, "lon", 1), around(first, "lon", -1)

    inputs = (
        vertical,
        alpha_fields,
        anomalies,
        lon_faces,
        lat_faces,
        normalizer,
        innovation,
        misfit_weight,
    )
    keep, give, alpha = pl.pallas_call(
        functools.partial(prepare_kernel, half),
        out_shape=(f32(6 * half, rows, lanes), f32(levels, rows, lanes), f32(*alpha_fields.shape)),
        in_specs=[HBM] * 8,
        out_specs=(VMEM, VMEM, VMEM),
        scratch_shapes=[
            pltpu.SMEM(vertical.shape, jnp.float32),
            pltpu.VMEM(anomalies.shape, jnp.float32),
            pltpu.VMEM(block.shape, jnp.float32),
            pltpu.VMEM(normalizer.shape, jnp.float32),
            pltpu.VMEM(block.shape, jnp.float32),
            pltpu.VMEM(misfit_weight.shape, jnp.float32),
            pltpu.SemaphoreType.DMA((8,)),
        ],
        compiler_params=PARAMS,
        name="prepare",
    )(*(pltpu.with_memory_space_constraint(value, pltpu.HBM) for value in inputs))
    got = around(give, "mem", 1)
    kept_below, kept_above = strips(keep, ((3 * half, DEEP), (2 * half, STEPS)), "kept_strips")
    got_below, got_above = strips(got, ((half, DEEP), (half, STEPS)), "got_strips")
    blocks = (keep, got, kept_below, got_below, kept_above, got_above)
    own_columns = pl.pallas_call(
        functools.partial(own_column_kernel, half),
        out_shape=(f32(groups, rows, lanes),) * 2,
        in_specs=[VMEM] * 2,
        out_specs=(VMEM,) * 2,
        compiler_params=PARAMS,
        name="own_columns",
    )(keep, got)
    early_columns = pl.pallas_call(
        functools.partial(early_column_kernel, half),
        out_shape=(f32(groups, 2, DEEP, lanes),) * 2,
        in_specs=[VMEM] * 2,
        out_specs=(VMEM,) * 2,
        compiler_params=PARAMS,
        name="early_columns",
    )(kept_below, kept_above)
    west, east = pl.pallas_call(
        functools.partial(column_kernel, half),
        out_shape=(column, column),
        in_specs=[VMEM] * 6,
        out_specs=(VMEM,) * 2,
        compiler_params=PARAMS,
        name="columns",
    )(*own_columns, *early_columns, got_below, got_above)
    left = around(east, "lat", 1)
    right = around(west, "lat", -1)
    edge_own = f32(high * 4 * half + (rows + 2 * STEPS) * 3 * half, lanes)
    main = pl.pallas_call(
        functools.partial(main_kernel, half),
        out_shape=(block, block, block, edge_own),
        in_specs=[VMEM] * 6,
        out_specs=(VMEM,) * 4,
        scratch_shapes=tiles,
        compiler_params=PARAMS,
        name="main",
    )(*blocks)
    total, mine, theirs = pl.pallas_call(
        functools.partial(edge_kernel, half),
        out_shape=(block, block, block),
        in_specs=[VMEM] * 6,
        out_specs=(VMEM,) * 3,
        scratch_shapes=[pltpu.VMEM(block.shape, jnp.float32)] + tiles,
        compiler_params=PARAMS,
        name="edge",
    )(left, right, *main)
    got = around(theirs, "mem", 1)

    partial, splat, increment = pl.pallas_call(
        functools.partial(partial_kernel, half),
        out_shape=(f32(levels, rows, lanes), f32(half, levels, lanes), block),
        in_specs=[SMEM] + [VMEM] * 4,
        out_specs=(VMEM,) * 3,
        compiler_params=PARAMS,
        name="partial",
    )(vertical, alpha, mine, keep, total)
    gradient = pl.pallas_call(
        functools.partial(gradient_kernel, half),
        out_shape=f32(*alpha_fields.shape),
        in_specs=[VMEM] * 3,
        out_specs=VMEM,
        compiler_params=PARAMS,
        name="gradient",
    )(partial, splat, got)
    return (increment, gradient)


def solution(mesh):
    return jax.shard_map(
        local,
        mesh=mesh,
        in_specs=(
            P("mem", None, "lon", "lat"),
            P("mem", None, "lon", "lat"),
            P(None, "lon", "lat"),
            P(None, "lon", "lat"),
            P(None, "lon", "lat"),
            P(None, "lon", "lat"),
            P(None, "lon", "lat"),
            P(),
        ),
        out_specs=(P("mem", "lon", "lat"), P("mem", None, "lon", "lat")),
        check_vma=False,
    )
```
